128 devices in a mesh: ctx: 16 (over z, y_hi, core), tp: 8 (over y_lo, x).
Axes of the slice: x: 4, y: 4 (y_hi: 2, y_lo: 2; y = y_hi * 2 + y_lo), z: 4, core: 2. Of those that a mesh axis runs over, the one named last changes fastest.
Arguments:
- queries: bfloat16 [1024, 128, 128], P('ctx', 'tp'), may hold values from -6 to 6
- cache_keys: bfloat16 [40960, 8, 128], P('ctx', 'tp'), may hold values from -6 to 6
- cache_values: bfloat16 [40960, 8, 128], P('ctx', 'tp'), may hold values from -6 to 6
- new_keys: bfloat16 [1024, 8, 128], P('ctx', 'tp'), may hold values from -6 to 6
- new_values: bfloat16 [1024, 8, 128], P('ctx', 'tp'), may hold values from -6 to 6
- cache_lengths: int32 [16], P('ctx'), may hold values from 640 to 2560, as said below
- causal_offset: int32 [1], replicated, may hold values from 20480 to 40959
- out_weight: bfloat16 [16384, 16384], P('tp', 'ctx'), may hold values from -0.046875 to 0.046875
Outputs:
- mixed: float32 [1024, 16384], P('tp', 'ctx')
The draws below stay inside these ranges and needn't reach their ends.
Inputs may be any that keep to these rules, and one draw needn't show every extreme that they name: `cache_lengths`: every shard has at least a quarter of its slots live; some shard is full.
All inputs are finite; a program needn't handle non-finite values.
Results may differ from the reference program's by a relative error of at most 0.013.
Values may be sent and summed in bfloat16 or wider, within the bound.
No kernel may reach another device: no remote copies, remote signals or barrier semaphores. Data moves between devices by JAX's collectives and lax.ppermute only.
A program may use at most 128 MiB of HBM per device.

```python
import math
import jax
import jax.numpy as jnp
from jax import lax

HEADS = 128
KVH = 8
HD = 128
D = 16384
CTX_DEV = 2560
NEW = 1024
CTX = 40960
N_CTX = 16


def draw_queries(key, part):
    key = jax.random.fold_in(key, 1)
    base_draw = jnp.clip(jax.random.normal(key, (NEW, HEADS, HD), jnp.float32), -4.0, 4.0)
    return base_draw.astype(jnp.bfloat16)


def draw_new_keys(key, part):
    key = jax.random.fold_in(key, 2)
    base_draw = jnp.clip(jax.random.normal(key, (NEW, KVH, HD), jnp.float32), -4.0, 4.0)
    return base_draw.astype(jnp.bfloat16)


def draw_cache_lengths(key, part):
    key = jax.random.fold_in(key, 3)
    key_len, key_full = jax.random.split(key)
    lengths = jax.random.randint(key_len, (N_CTX,), CTX_DEV // 4, CTX_DEV + 1)
    full_shard = jax.random.randint(key_full, (), 0, N_CTX)
    return lengths.at[full_shard].set(CTX_DEV).astype(jnp.int32)


def steps_of(stream_key, extent, pieces, smallest, top_value):
    loudness = 1.0
    for axis_at, parts in pieces:
        draws = jax.random.uniform(jax.random.fold_in(jax.random.fold_in(stream_key, 6), axis_at), (parts,), jnp.float32, smallest / len(pieces), top_value / len(pieces))
        loudness = loudness * jnp.repeat(jnp.exp(draws), extent[axis_at] // parts).reshape((-1,) + (1,) * (len(extent) - 1 - axis_at))
    return loudness


def noise(key, shape, scale, reach, cuts=(), kind=jnp.bfloat16):
    values = scale * jax.random.normal(key, shape, jnp.float32)
    if cuts:
        values = values * steps_of(key, shape, cuts, -0.22, 0.18)
    return jnp.clip(values, -reach, reach).astype(kind)


def setup_inputs(seed: int = 0) -> dict:
    splits = jax.random.split(jax.random.key(seed), 9)
    queries = draw_queries(jax.random.fold_in(splits[8], 71), 0)
    cache_keys = noise(splits[1], (CTX, KVH, HD), 1.0, 6.0, ((0, 16), (1, 8)))
    cache_values = noise(splits[2], (CTX, KVH, HD), 1.0, 6.0, ((0, 16), (1, 8)))
    new_keys = draw_new_keys(jax.random.fold_in(splits[8], 71), 0)
    new_values = noise(splits[4], (NEW, KVH, HD), 1.0, 6.0, ((0, 16), (1, 8)))
    cache_lengths = draw_cache_lengths(jax.random.fold_in(splits[8], 71), 0)
    causal_offset = jax.random.randint(splits[6], (1,), CTX // 2, CTX).astype(jnp.int32)
    out_weight = noise(splits[7], (HEADS * HD, D), (HEADS * HD) ** -0.5, 0.046875, ((0, 8), (1, 16)))
    return dict(queries=queries, cache_keys=cache_keys, cache_values=cache_values, new_keys=new_keys, new_values=new_values, cache_lengths=cache_lengths, causal_offset=causal_offset, out_weight=out_weight)


def reference(queries, cache_keys, cache_values, new_keys, new_values, cache_lengths, causal_offset, out_weight):
    head_group = HEADS // KVH
    score_scale = 1.0 / math.sqrt(HD)
    cache_slot = jnp.arange(CTX_DEV, dtype=jnp.int32)
    shard_index = jnp.arange(N_CTX, dtype=jnp.int32)
    cache_pos = (shard_index[:, None] * CTX_DEV + cache_slot[None, :]).reshape(-1)
    cache_live = (cache_slot[None, :] < cache_lengths[:, None]).reshape(-1)
    token_index = jnp.arange(NEW, dtype=jnp.int32)
    cache_seen = cache_live[None, :] & (cache_pos[None, :] <= causal_offset[0] + token_index[:, None])
    new_seen = token_index[None, :] <= token_index[:, None]
    visible = jnp.concatenate([cache_seen, new_seen], axis=1)
    all_keys = jnp.concatenate([cache_keys, new_keys], axis=0)
    all_values = jnp.concatenate([cache_values, new_values], axis=0)

    def one_head(head):
        kv_head = head // head_group
        query_rows = queries[:, head, :]
        key_rows = all_keys[:, kv_head, :]
        value_rows = all_values[:, kv_head, :]
        scores = jnp.dot(query_rows, key_rows.T, preferred_element_type=jnp.float32) * score_scale
        scores = jnp.where(visible, scores, -1e+30)
        row_max = lax.optimization_barrier(jnp.max(scores, axis=1, keepdims=True))
        weights = jnp.where(visible, jnp.exp(scores - row_max), 0.0)
        row_sum = lax.optimization_barrier(jnp.sum(weights, axis=1, keepdims=True))
        output = jnp.dot(weights.astype(jnp.bfloat16), value_rows, preferred_element_type=jnp.float32) / row_sum
        return output.astype(jnp.bfloat16)
    per_head = lax.map(one_head, jnp.arange(HEADS, dtype=jnp.int32))
    attended = jnp.transpose(per_head, (1, 0, 2)).reshape(NEW, HEADS * HD)
    return jnp.dot(attended, out_weight, preferred_element_type=jnp.float32)
```

```python
import functools
import math

import jax
import jax.numpy as jnp
from jax import lax
from jax.experimental import pallas as pl
from jax.experimental.pallas import tpu as pltpu
from jax.sharding import PartitionSpec as P

LOG2E = math.log2(math.e)
FAR = -1e30
NEVER = 1 << 30
CUT = 256
SMALL = 512
LARGE = 1024
VM = pl.BlockSpec(memory_space=pltpu.VMEM)
SM = pl.BlockSpec(memory_space=pltpu.SMEM)
CALLS = (((0, 0), (0, 1)), ((2, 0), (2, 1)), ((1, 0), (3, 0)), ((1, 1), (3, 1)))
OTHERS = tuple(rel for call in CALLS for rel in call if rel != (0, 0))


def up16(n):
    return (n + 15) // 16 * 16


def spans(facts, slots, tokens):
    seen = [
        jnp.clip(jnp.minimum(facts[1 + s], facts[0] + tokens - facts[3 + s] * slots), 0, slots)
        for s in (0, 1)
    ]
    return seen, up16(seen[0]), up16(seen[1])


def pack_kernel(
    tokens, facts, k0, k1, v0, v1, nk0, nk1, nv0, nv1, keys_ref, values_ref, pos_ref
):
    slots = k0.shape[0]
    fresh = nk0.shape[0]
    (n0, n1), c0, c1 = spans(facts, slots, tokens)
    for out, a, b, c, d in ((keys_ref, k0, k1, nk0, nk1), (values_ref, v0, v1, nv0, nv1)):
        out[:slots, :] = a[...]
        out[pl.ds(pl.multiple_of(c0, 16), slots), :] = b[...]
        at = pl.multiple_of(c0 + c1, 16)
        out[pl.ds(at, fresh), :] = c[...]
        at = pl.multiple_of(c0 + c1 + fresh, 16)
        out[pl.ds(at, fresh), :] = d[...]
        at = pl.multiple_of(c0 + c1 + 2 * fresh, 16)
        out[pl.ds(at, SMALL), :] = jnp.zeros((SMALL, out.shape[1]), out.dtype)
    j = lax.broadcasted_iota(jnp.int32, pos_ref.shape, 1)
    one = j - c0
    two = one - c1
    three = two - fresh
    pos = jnp.where(j < n0, facts[3] * slots + j, NEVER)
    pos = jnp.where(j >= c0, jnp.where(one < n1, facts[4] * slots + one, NEVER), pos)
    pos = jnp.where(two >= 0, facts[0] + facts[3] * fresh + two, pos)
    pos = jnp.where(three >= 0, facts[0] + facts[4] * fresh + three, pos)
    pos = jnp.where(three >= fresh, NEVER, pos)
    pos_ref[...] = pos


def pack(facts, k0, k1, v0, v1, nk0, nk1, nv0, nv1, tokens):
    slots, depth = k0.shape
    size = 2 * slots + 2 * nk0.shape[0] + SMALL
    return pl.pallas_call(
        functools.partial(pack_kernel, tokens),
        out_shape=(
            jax.ShapeDtypeStruct((size, depth), k0.dtype),
            jax.ShapeDtypeStruct((size, depth), k0.dtype),
            jax.ShapeDtypeStruct((1, size), jnp.int32),
        ),
        in_specs=[SM] + [VM] * 8,
        out_specs=(VM, VM, VM),
        compiler_params=pltpu.CompilerParams(vmem_limit_bytes=16 << 20),
        cost_estimate=pl.CostEstimate(
            flops=0, bytes_accessed=8 * slots * depth * 2, transcendentals=0
        ),
    )(facts, k0, k1, v0, v1, nk0, nk1, nv0, nv1)


def attend_kernel(all_tokens, slots, n_chunk, facts, firsts, *refs):
    q_refs, refs = refs[:n_chunk], refs[n_chunk:]
    keys_ref, values_ref, pos_ref = refs[:3]
    out_refs, (q2, acc, top) = refs[3 : 3 + n_chunk], refs[3 + n_chunk :]
    heads, tokens, depth = q_refs[0].shape
    rows = heads * tokens
    scale = LOG2E / math.sqrt(depth)
    (n0, n1), c0, c1 = spans(facts, slots, all_tokens)
    count = (c0 + c1 + 2 * tokens + SMALL - 1) // SMALL
    token = lax.broadcasted_iota(jnp.int32, (tokens, 128), 0)
    lasts = [
        jnp.concatenate([token + (facts[0] + firsts[c])] * (CUT // tokens), 0)
        for c in range(n_chunk)
    ]
    starts = [(c, r) for c in range(n_chunk) for r in range(0, rows, CUT)]

    def hide(scores, pos, last):
        return jnp.concatenate(
            [
                jnp.where(pos[:, at : at + 128] <= last, scores[:, at : at + 128], FAR)
                for at in range(0, scores.shape[1], 128)
            ],
            1,
        )

    def contract(left, right):
        return lax.dot_general(
            left, right, (((1,), (1,)), ((), ())), preferred_element_type=jnp.float32
        )

    def block_at(start, size):
        here = pl.ds(pl.multiple_of(start, SMALL), size)
        values = values_ref[here, :]
        return (
            keys_ref[here, :],
            jnp.concatenate([values, jnp.ones_like(values)], 1),
            pos_ref[:, here],
        )

    for c, r in starts:
        scaled = q_refs[c][r // tokens : (r + CUT) // tokens].reshape(CUT, depth)
        scaled = scaled.astype(jnp.float32) * scale
        high = scaled.astype(jnp.bfloat16)
        q2[c, r : r + CUT, :depth] = high
        q2[c, r : r + CUT, depth:] = (scaled - high.astype(jnp.float32)).astype(jnp.bfloat16)
    acc[...] = jnp.zeros_like(acc)

    def step(start, size):
        keys, values, pos = block_at(start, size)
        keys = jnp.concatenate([keys, keys], 1)
        for c, r in starts:
            scores = hide(contract(q2[c, r : r + CUT, :], keys), pos, lasts[c])
            acc[c, r : r + CUT, :] += jnp.dot(
                jnp.exp2(scores).astype(jnp.bfloat16), values, preferred_element_type=jnp.float32
            )

    def large_step(at, _):
        step(at * LARGE, LARGE)
        return 0

    lax.fori_loop(0, count // 2, large_step, 0)

    @pl.when(count % 2 == 1)
    def _():
        step((count - 1) * SMALL, SMALL)

    groups = rows // 128
    eye = lax.broadcasted_iota(jnp.int32, (128, 128), 0) == lax.broadcasted_iota(
        jnp.int32, (128, 128), 1
    )

    def dense(ref, c, at):
        lines = []
        for g in range(groups):
            square = ref[c, g * 128 : (g + 1) * 128, at : at + 128]
            lines.append(jnp.sum(jnp.where(eye, square, 0.0), axis=0, keepdims=True))
        return jnp.concatenate(lines, 0)

    who = lax.broadcasted_iota(jnp.int32, (groups, 128), 1) % tokens
    wrong = jnp.zeros((groups, 128), jnp.float32)
    for c in range(n_chunk):
        total = dense(acc, c, depth)
        mine = who + firsts[c]
        seen = mine >= facts[3] * tokens
        for s, n in ((0, n0), (1, n1)):
            seen = seen | ((n > 0) & (mine + facts[0] >= facts[3 + s] * slots))
        sound = (total > 2.0**-100) & (total < 2.0**120)
        wrong = jnp.maximum(wrong, jnp.where(seen & ~sound, 1.0, 0.0))
    top[...] = jnp.zeros_like(top)

    @pl.when(jnp.max(wrong) > 0.0)
    def _():
        acc[...] = jnp.zeros_like(acc)
        top[...] = jnp.full_like(top, FAR)
        cuts = rows // CUT
        for c in range(n_chunk):

            def slow_step(i, _):
                at, r = i // cuts, i % cuts
                keys, values, pos = block_at(at * SMALL, SMALL)
                per = CUT // tokens
                query = q_refs[c][pl.ds(r * per, per)].reshape(CUT, depth)
                scores = hide(contract(query, keys) * scale, pos, lasts[c])
                here = pl.ds(pl.multiple_of(r * CUT, CUT), CUT)
                old = top[c, here, :]
                peak = jnp.maximum(old, jnp.max(scores, axis=1, keepdims=True))
                top[c, here, :] = peak
                part = jnp.where(scores > FAR * 0.5, jnp.exp2(scores - peak[:, :1]), 0.0)
                fade = jnp.exp2(old - peak)
                acc[c, here, :] = acc[c, here, :] * jnp.concatenate([fade, fade], 1) + jnp.dot(
                    part.astype(jnp.bfloat16), values, preferred_element_type=jnp.float32
                )
                return 0

            lax.fori_loop(0, count * cuts, slow_step, 0)

    for c, r in starts:
        some = acc[c, r : r + CUT, depth:]
        out_refs[c][r : r + CUT, :] = (
            acc[c, r : r + CUT, :depth] / jnp.where(some > 0.0, some, 1.0)
        ).astype(jnp.bfloat16)
    for c in range(n_chunk):
        total = dense(acc, c, depth)
        level = jnp.where(
            total > 0.0,
            dense(top, c, 0) + jnp.log2(jnp.where(total > 0.0, total, 1.0)),
            FAR,
        )
        pieces = []
        for _ in range(3):
            pieces.append(level.astype(jnp.bfloat16).astype(jnp.float32))
            level = level - pieces[-1]
        pieces.append(jnp.zeros_like(level))
        tail = jnp.concatenate(pieces, 0)
        out_refs[c][rows : rows + 4 * groups, :] = tail.astype(jnp.bfloat16)


def attend(facts, firsts, queries, keys, values, pos, slots, all_tokens):
    heads, tokens, depth = queries[0].shape
    rows = heads * tokens
    n = len(queries)
    return pl.pallas_call(
        functools.partial(attend_kernel, all_tokens, slots, n),
        out_shape=[jax.ShapeDtypeStruct((rows + rows // 32, depth), jnp.bfloat16)] * n,
        in_specs=[SM, SM] + [VM] * (n + 3),
        out_specs=[VM] * n,
        scratch_shapes=[
            pltpu.VMEM((n, rows, 2 * depth), jnp.bfloat16),
            pltpu.VMEM((n, rows, 2 * depth), jnp.float32),
            pltpu.VMEM((n, rows, depth), jnp.float32),
        ],
        compiler_params=pltpu.CompilerParams(vmem_limit_bytes=28 << 20),
        cost_estimate=pl.CostEstimate(
            flops=8 * rows * n * keys.shape[0] * depth,
            bytes_accessed=4 * keys.shape[0] * depth,
            transcendentals=0,
        ),
    )(facts, firsts, *queries, keys, values, pos)


def merge_kernel(*refs):
    parts, out_ref = refs[:-1], refs[-1]
    tokens = out_ref.shape[0]
    depth = parts[0].shape[1]
    rows = tokens * out_ref.shape[1] // depth
    groups = rows // 128
    levels = []
    for part in parts:
        tail = part[rows : rows + 4 * groups, :].astype(jnp.float32)
        levels.append(
            tail[:groups] + tail[groups : 2 * groups] + tail[2 * groups : 3 * groups]
        )
    peak = functools.reduce(jnp.maximum, levels)
    shares = [jnp.exp2(level - peak) for level in levels]
    total = functools.reduce(jnp.add, shares)
    shares = [share / total for share in shares]
    eye = lax.broadcasted_iota(jnp.int32, (128, 128), 0) == lax.broadcasted_iota(
        jnp.int32, (128, 128), 1
    )
    for g in range(groups):
        mix, blocks = [], []
        for share, part in zip(shares, parts):
            square = jnp.where(eye, share[g : g + 1, :], 0.0)
            high = square.astype(jnp.bfloat16)
            mix += [high, (square - high.astype(jnp.float32)).astype(jnp.bfloat16)]
            block = part[g * 128 : (g + 1) * 128, :]
            blocks += [block, block]
        merged = jnp.dot(
            jnp.concatenate(mix, 1), jnp.concatenate(blocks, 0), preferred_element_type=jnp.float32
        ).astype(out_ref.dtype)
        for i in range(128 // tokens):
            head = g * (128 // tokens) + i
            out_ref[:, head * depth : (head + 1) * depth] = merged[i * tokens : (i + 1) * tokens]


def merge(parts, tokens, width):
    return pl.pallas_call(
        merge_kernel,
        out_shape=jax.ShapeDtypeStruct((tokens, width), jnp.bfloat16),
        in_specs=[VM] * len(parts),
        out_specs=VM,
        compiler_params=pltpu.CompilerParams(vmem_limit_bytes=16 << 20),
        cost_estimate=pl.CostEstimate(
            flops=1 << 22, bytes_accessed=9 * tokens * width * 2, transcendentals=0
        ),
    )(*parts)


def project_kernel(n_block, spots, *refs):
    blocks, weight_ref = refs[:n_block], refs[n_block]
    out_refs = refs[n_block + 1 : -2]
    all_rows, mixed = refs[-2:]
    tokens = blocks[0].shape[0]
    for i, block in enumerate(blocks):
        all_rows[pl.ds(pl.multiple_of(spots[i] * tokens, tokens), tokens), :] = block[...]
    width = weight_ref.shape[1]
    for at in range(0, width, 256):
        mixed[:, at : at + 256] = jnp.dot(
            all_rows[...], weight_ref[:, at : at + 256], preferred_element_type=jnp.float32
        ).astype(mixed.dtype)
    tall = out_refs[0].shape[0]
    for i, out in enumerate(out_refs):
        out[...] = mixed[pl.ds(pl.multiple_of(spots[n_block + i] * tall, tall), tall), :]


def project(spots, blocks, weight, n_out):
    tokens, width = blocks[0].shape
    total = tokens * len(blocks)
    cols = weight.shape[1]
    return pl.pallas_call(
        functools.partial(project_kernel, len(blocks)),
        out_shape=[jax.ShapeDtypeStruct((total // n_out, cols), jnp.bfloat16)] * n_out,
        in_specs=[SM] + [VM] * (len(blocks) + 1),
        out_specs=[VM] * n_out,
        scratch_shapes=[
            pltpu.VMEM((total, width), jnp.bfloat16),
            pltpu.VMEM((total, cols), jnp.bfloat16),
        ],
        compiler_params=pltpu.CompilerParams(vmem_limit_bytes=28 << 20),
        cost_estimate=pl.CostEstimate(
            flops=2 * total * width * cols,
            bytes_accessed=2 * (total * width + width * cols + total * cols),
            transcendentals=0,
        ),
    )(spots, *blocks, weight)


def chip_at(index, rel):
    z, y, core = index // 4, index // 2 % 2, index % 2
    return ((z + rel[0]) % 4 * 2 + (y + rel[1]) % 2) * 2 + core


def fetch(block, rel, count):
    return lax.ppermute(block, "ctx", [(chip_at(i, rel), i) for i in range(count)])


def deliver(block, rel, count):
    return lax.ppermute(block, "ctx", [(i, chip_at(i, rel)) for i in range(count)])


def local(
    queries, cache_keys, cache_values, new_keys, new_values, cache_lengths, causal_offset, out_weight
):
    tokens, heads, depth = queries.shape
    slots = cache_keys.shape[0]
    ctx_count = lax.axis_size("ctx")
    tp_count = lax.axis_size("tp")
    ctx_index = lax.axis_index("ctx")
    tp_index = lax.axis_index("tp")
    all_tokens = tokens * ctx_count

    def swap(block):
        return lax.ppermute(block, "ctx", [(i, i ^ 1) for i in range(ctx_count)])

    mine = [
        cache_keys.reshape(slots, depth),
        cache_values.reshape(slots, depth),
        new_keys.reshape(tokens, depth),
        new_values.reshape(tokens, depth),
    ]
    theirs = [swap(block) for block in mine]
    lengths = [cache_lengths, swap(cache_lengths)]
    places = [ctx_index, ctx_index ^ 1]
    facts = jnp.stack(
        [causal_offset[0], lengths[0][0], lengths[1][0], places[0], places[1]]
    ).astype(jnp.int32)

    own = jnp.transpose(queries, (1, 0, 2))
    held = {(0, 0): own, (0, 1): fetch(own, (0, 1), ctx_count)}
    for rel in OTHERS[1:]:
        held[rel] = fetch(held[(0, rel[1])], (rel[0], 0), ctx_count)

    packed = pack(
        facts, mine[0], theirs[0], mine[1], theirs[1], mine[2], theirs[2], mine[3], theirs[3],
        all_tokens,
    )
    parts = []
    for call in CALLS:
        firsts = jnp.stack([chip_at(ctx_index, rel) * tokens for rel in call]).astype(jnp.int32)
        made = attend(facts, firsts, [held[rel] for rel in call], *packed, slots, all_tokens)
        for rel, part in zip(call, made):
            parts.append(part if rel == (0, 0) else deliver(part, rel, ctx_count))
    attended = merge(parts, tokens, heads * depth)

    blocks, spots = [], []
    for rel in ((0, 0),) + OTHERS:
        block = attended if rel == (0, 0) else fetch(attended, rel, ctx_count)
        blocks += [block, swap(block)]
        at = chip_at(ctx_index, rel)
        spots += [at, at ^ 1]
    spots += [tp_index ^ i for i in range(tp_count)]
    mixed = project(jnp.stack(spots).astype(jnp.int32), blocks, out_weight, tp_count)
    total = mixed[0].astype(jnp.float32)
    for i in range(1, tp_count):
        sent = lax.ppermute(mixed[i], "tp", [(j, j ^ i) for j in range(tp_count)])
        total = total + sent.astype(jnp.float32)
    return total


def solution(mesh):
    return jax.shard_map(
        local,
        mesh=mesh,
        in_specs=(
            P("ctx", "tp", None),
            P("ctx", "tp", None),
            P("ctx", "tp", None),
            P("ctx", "tp", None),
            P("ctx", "tp", None),
            P("ctx"),
            P(),
            P("tp", "ctx"),
        ),
        out_specs=P("tp", "ctx"),
        check_vma=False,
    )
```

```python
import functools
import math

import jax
import jax.numpy as jnp
from jax import lax
from jax.experimental import pallas as pl
from jax.experimental.pallas import tpu as pltpu
from jax.sharding import PartitionSpec as P

LOG2E = math.log2(math.e)
FAR = -1e30
NEVER = 1 << 30
CUT = 256
SMALL = 512
LARGE = 1024
VM = pl.BlockSpec(memory_space=pltpu.VMEM)
SM = pl.BlockSpec(memory_space=pltpu.SMEM)
CALLS = (((1, 0), (3, 0)), ((2, 0), (1, 1)), ((3, 1), (2, 1)), ((0, 1),), ((0, 0),))
OTHERS = tuple(rel for call in CALLS for rel in call if rel != (0, 0))


def up16(n):
    return (n + 15) // 16 * 16


def spans(facts, slots, tokens):
    seen = [
        jnp.clip(jnp.minimum(facts[1 + s], facts[0] + tokens - facts[3 + s] * slots), 0, slots)
        for s in (0, 1)
    ]
    return seen, up16(seen[0]), up16(seen[1])


def pack_kernel(
    tokens, facts, k0, k1, v0, v1, new0, new1, keys_ref, values_ref, pos_ref, sems
):
    slots = k0.shape[0]
    fresh = (new0.shape[0] - 16) // 2
    (n0, n1), c0, c1 = spans(facts, slots, tokens)
    outs = (keys_ref, values_ref)

    def move(pieces):
        copies = [
            pltpu.make_async_copy(src, out.at[pl.ds(at, src.shape[0]), :], sems.at[i])
            for i, (src, out, at) in enumerate(pieces)
        ]
        for copy in copies:
            copy.start()
        for copy in copies:
            copy.wait()

    move([(src, out, 0) for src, out in zip((k0, v0), outs)])
    at = pl.multiple_of(c0, 16)
    move([(src, out, at) for src, out in zip((k1, v1), outs)])
    for i, out in enumerate(outs):
        for j, new in enumerate((new0, new1)):
            at = pl.multiple_of(c0 + c1 + j * fresh, 16)
            out[pl.ds(at, fresh), :] = new[i * fresh : (i + 1) * fresh, :]
        at = pl.multiple_of(c0 + c1 + 2 * fresh, 16)
        out[pl.ds(at, SMALL), :] = jnp.zeros((SMALL, out.shape[1]), out.dtype)
    j = lax.broadcasted_iota(jnp.int32, pos_ref.shape, 1)
    one = j - c0
    two = one - c1
    three = two - fresh
    pos = jnp.where(j < n0, facts[3] * slots + j, NEVER)
    pos = jnp.where(j >= c0, jnp.where(one < n1, facts[4] * slots + one, NEVER), pos)
    pos = jnp.where(two >= 0, facts[0] + facts[3] * fresh + two, pos)
    pos = jnp.where(three >= 0, facts[0] + facts[4] * fresh + three, pos)
    pos = jnp.where(three >= fresh, NEVER, pos)
    pos_ref[...] = pos


def pack(facts, k0, k1, v0, v1, new0, new1, tokens):
    slots, depth = k0.shape
    size = 2 * slots + new0.shape[0] - 16 + SMALL
    anywhere = pl.BlockSpec(memory_space=pl.ANY)
    return pl.pallas_call(
        functools.partial(pack_kernel, tokens),
        out_shape=(
            jax.ShapeDtypeStruct((size, depth), k0.dtype),
            jax.ShapeDtypeStruct((size, depth), k0.dtype),
            jax.ShapeDtypeStruct((1, size), jnp.int32),
        ),
        in_specs=[SM] + [anywhere] * 4 + [VM] * 2,
        out_specs=(VM, VM, VM),
        scratch_shapes=[pltpu.SemaphoreType.DMA((2,))],
        compiler_params=pltpu.CompilerParams(vmem_limit_bytes=16 << 20),
        cost_estimate=pl.CostEstimate(
            flops=0, bytes_accessed=8 * slots * depth * 2, transcendentals=0
        ),
    )(facts, k0, k1, v0, v1, new0, new1)


def attend_kernel(all_tokens, slots, skips, heads, facts, firsts, *refs):
    n_chunk = len(skips)
    q_refs, refs = refs[:n_chunk], refs[n_chunk:]
    keys_ref, values_ref, pos_ref = refs[:3]
    out_refs, (q2, acc, top) = refs[3 : 3 + n_chunk], refs[3 + n_chunk :]
    _, tokens, depth = q_refs[0].shape
    rows = heads * tokens
    scale = LOG2E / math.sqrt(depth)
    (n0, n1), c0, c1 = spans(facts, slots, all_tokens)
    count = (c0 + c1 + 2 * tokens + SMALL - 1) // SMALL
    token = lax.broadcasted_iota(jnp.int32, (tokens, 128), 0)
    lasts = [
        jnp.concatenate([token + (facts[0] + firsts[c])] * (CUT // tokens), 0)
        for c in range(n_chunk)
    ]
    starts = [(c, r) for c in range(n_chunk) for r in range(0, rows, CUT)]

    def hide(scores, pos, last):
        return jnp.concatenate(
            [
                jnp.where(pos[:, at : at + 128] <= last, scores[:, at : at + 128], FAR)
                for at in range(0, scores.shape[1], 128)
            ],
            1,
        )

    def contract(left, right):
        return lax.dot_general(
            left, right, (((1,), (1,)), ((), ())), preferred_element_type=jnp.float32
        )

    def block_at(start, size):
        here = pl.ds(pl.multiple_of(start, SMALL), size)
        values = values_ref[here, :]
        return (
            keys_ref[here, :],
            jnp.concatenate([values, jnp.ones_like(values)], 1),
            pos_ref[:, here],
        )

    for c, r in starts:
        at = skips[c] * heads + r // tokens
        scaled = q_refs[c][at : at + CUT // tokens].reshape(CUT, depth)
        scaled = scaled.astype(jnp.float32) * scale
        high = scaled.astype(jnp.bfloat16)
        q2[c, r : r + CUT, :depth] = high
        q2[c, r : r + CUT, depth:] = (scaled - high.astype(jnp.float32)).astype(jnp.bfloat16)
    acc[...] = jnp.zeros_like(acc)

    def step(start, size):
        keys, values, pos = block_at(start, size)
        keys = jnp.concatenate([keys, keys], 1)
        for c, r in starts:
            scores = hide(contract(q2[c, r : r + CUT, :], keys), pos, lasts[c])
            acc[c, r : r + CUT, :] += jnp.dot(
                jnp.exp2(scores).astype(jnp.bfloat16), values, preferred_element_type=jnp.float32
            )

    def large_step(at, _):
        step(at * LARGE, LARGE)
        return 0

    lax.fori_loop(0, count // 2, large_step, 0)

    @pl.when(count % 2 == 1)
    def _():
        step((count - 1) * SMALL, SMALL)

    groups = rows // 128
    eye = lax.broadcasted_iota(jnp.int32, (128, 128), 0) == lax.broadcasted_iota(
        jnp.int32, (128, 128), 1
    )

    def dense(ref, c, at):
        lines = []
        for g in range(groups):
            square = ref[c, g * 128 : (g + 1) * 128, at : at + 128]
            lines.append(jnp.sum(jnp.where(eye, square, 0.0), axis=0, keepdims=True))
        return jnp.concatenate(lines, 0)

    who = lax.broadcasted_iota(jnp.int32, (groups, 128), 1) % tokens
    wrong = jnp.zeros((groups, 128), jnp.float32)
    for c in range(n_chunk):
        total = dense(acc, c, depth)
        mine = who + firsts[c]
        seen = mine >= facts[3] * tokens
        for s, n in ((0, n0), (1, n1)):
            seen = seen | ((n > 0) & (mine + facts[0] >= facts[3 + s] * slots))
        sound = (total > 2.0**-100) & (total < 2.0**120)
        wrong = jnp.maximum(wrong, jnp.where(seen & ~sound, 1.0, 0.0))
    top[...] = jnp.zeros_like(top)

    @pl.when(jnp.max(wrong) > 0.0)
    def _():
        acc[...] = jnp.zeros_like(acc)
        top[...] = jnp.full_like(top, FAR)
        cuts = rows // CUT
        for c in range(n_chunk):

            def slow_step(i, _):
                at, r = i // cuts, i % cuts
                keys, values, pos = block_at(at * SMALL, SMALL)
                per = CUT // tokens
                query = q_refs[c][pl.ds(skips[c] * heads + r * per, per)].reshape(CUT, depth)
                scores = hide(contract(query, keys) * scale, pos, lasts[c])
                here = pl.ds(pl.multiple_of(r * CUT, CUT), CUT)
                old = top[c, here, :]
                peak = jnp.maximum(old, jnp.max(scores, axis=1, keepdims=True))
                top[c, here, :] = peak
                part = jnp.where(scores > FAR * 0.5, jnp.exp2(scores - peak[:, :1]), 0.0)
                fade = jnp.exp2(old - peak)
                acc[c, here, :] = acc[c, here, :] * jnp.concatenate([fade, fade], 1) + jnp.dot(
                    part.astype(jnp.bfloat16), values, preferred_element_type=jnp.float32
                )
                return 0

            lax.fori_loop(0, count * cuts, slow_step, 0)

    for c, r in starts:
        some = acc[c, r : r + CUT, depth:]
        out_refs[c][r : r + CUT, :] = (
            acc[c, r : r + CUT, :depth] / jnp.where(some > 0.0, some, 1.0)
        ).astype(jnp.bfloat16)
    for c in range(n_chunk):
        total = dense(acc, c, depth)
        level = jnp.where(
            total > 0.0,
            dense(top, c, 0) + jnp.log2(jnp.where(total > 0.0, total, 1.0)),
            FAR,
        )
        pieces = []
        for _ in range(3):
            pieces.append(level.astype(jnp.bfloat16).astype(jnp.float32))
            level = level - pieces[-1]
        pieces.append(jnp.zeros_like(level))
        tail = jnp.concatenate(pieces, 0)
        out_refs[c][rows : rows + 4 * groups, :] = tail.astype(jnp.bfloat16)


def attend(facts, firsts, queries, skips, heads, keys, values, pos, slots, all_tokens):
    _, tokens, depth = queries[0].shape
    rows = heads * tokens
    n = len(queries)
    return pl.pallas_call(
        functools.partial(attend_kernel, all_tokens, slots, skips, heads),
        out_shape=[jax.ShapeDtypeStruct((rows + rows // 32, depth), jnp.bfloat16)] * n,
        in_specs=[SM, SM] + [VM] * (n + 3),
        out_specs=[VM] * n,
        scratch_shapes=[
            pltpu.VMEM((n, rows, 2 * depth), jnp.bfloat16),
            pltpu.VMEM((n, rows, 2 * depth), jnp.float32),
            pltpu.VMEM((n, rows, depth), jnp.float32),
        ],
        compiler_params=pltpu.CompilerParams(vmem_limit_bytes=28 << 20),
        cost_estimate=pl.CostEstimate(
            flops=8 * rows * n * keys.shape[0] * depth,
            bytes_accessed=4 * keys.shape[0] * depth,
            transcendentals=0,
        ),
    )(facts, firsts, *queries, keys, values, pos)


def merge_kernel(*refs):
    parts, out_ref = refs[:-1], refs[-1]
    tokens = out_ref.shape[0]
    depth = parts[0].shape[1]
    rows = tokens * out_ref.shape[1] // depth
    groups = rows // 128
    levels = []
    for part in parts:
        tail = part[rows : rows + 4 * groups, :].astype(jnp.float32)
        levels.append(
            tail[:groups] + tail[groups : 2 * groups] + tail[2 * groups : 3 * groups]
        )
    peak = functools.reduce(jnp.maximum, levels)
    shares = [jnp.exp2(level - peak) for level in levels]
    total = functools.reduce(jnp.add, shares)
    shares = [share / total for share in shares]
    eye = lax.broadcasted_iota(jnp.int32, (128, 128), 0) == lax.broadcasted_iota(
        jnp.int32, (128, 128), 1
    )
    for g in range(groups):
        mix, blocks = [], []
        for share, part in zip(shares, parts):
            square = jnp.where(eye, share[g : g + 1, :], 0.0)
            high = square.astype(jnp.bfloat16)
            mix += [high, (square - high.astype(jnp.float32)).astype(jnp.bfloat16)]
            block = part[g * 128 : (g + 1) * 128, :]
            blocks += [block, block]
        merged = jnp.dot(
            jnp.concatenate(mix, 1), jnp.concatenate(blocks, 0), preferred_element_type=jnp.float32
        ).astype(out_ref.dtype)
        for i in range(128 // tokens):
            head = g * (128 // tokens) + i
            out_ref[:, head * depth : (head + 1) * depth] = merged[i * tokens : (i + 1) * tokens]


def merge(parts, tokens, width):
    return pl.pallas_call(
        merge_kernel,
        out_shape=jax.ShapeDtypeStruct((tokens, width), jnp.bfloat16),
        in_specs=[VM] * len(parts),
        out_specs=VM,
        compiler_params=pltpu.CompilerParams(vmem_limit_bytes=16 << 20),
        cost_estimate=pl.CostEstimate(
            flops=1 << 22, bytes_accessed=9 * tokens * width * 2, transcendentals=0
        ),
    )(*parts)


def project_kernel(n_block, spots, *refs):
    blocks, weight_ref = refs[:n_block], refs[n_block]
    out_refs = refs[n_block + 1 : -2]
    all_rows, mixed = refs[-2:]
    tokens = blocks[0].shape[0]

    @pl.when(pl.program_id(0) == 0)
    def _():
        for i, block in enumerate(blocks):
            here = pl.ds(pl.multiple_of(spots[i] * tokens, tokens), tokens)
            all_rows[here, :] = block[...]

    mixed[...] = jnp.dot(
        all_rows[...], weight_ref[...], preferred_element_type=jnp.float32
    ).astype(mixed.dtype)
    tall = out_refs[0].shape[0]
    for i, out in enumerate(out_refs):
        out[...] = mixed[pl.ds(pl.multiple_of(spots[n_block + i] * tall, tall), tall), :]


def project(spots, blocks, weight, n_out):
    tokens, width = blocks[0].shape
    total = tokens * len(blocks)
    cols = weight.shape[1]
    wide = 256
    return pl.pallas_call(
        functools.partial(project_kernel, len(blocks)),
        grid=(cols // wide,),
        out_shape=[jax.ShapeDtypeStruct((total // n_out, cols), jnp.bfloat16)] * n_out,
        in_specs=[SM] + [VM] * len(blocks) + [pl.BlockSpec((width, wide), lambda i: (0, i))],
        out_specs=[pl.BlockSpec((total // n_out, wide), lambda i: (0, i))] * n_out,
        scratch_shapes=[
            pltpu.VMEM((total, width), jnp.bfloat16),
            pltpu.VMEM((total, wide), jnp.bfloat16),
        ],
        compiler_params=pltpu.CompilerParams(vmem_limit_bytes=28 << 20),
        cost_estimate=pl.CostEstimate(
            flops=2 * total * width * cols,
            bytes_accessed=2 * (total * width + width * cols + total * cols),
            transcendentals=0,
        ),
    )(spots, *blocks, weight)


def chip_at(index, rel):
    z, y, core = index // 4, index // 2 % 2, index % 2
    return ((z + rel[0]) % 4 * 2 + (y + rel[1]) % 2) * 2 + core


def fetch(block, rel, count):
    return lax.ppermute(block, "ctx", [(chip_at(i, rel), i) for i in range(count)])


def deliver(block, rel, count):
    return lax.ppermute(block, "ctx", [(i, chip_at(i, rel)) for i in range(count)])


def local(
    queries, cache_keys, cache_values, new_keys, new_values, cache_lengths, causal_offset, out_weight
):
    tokens, heads, depth = queries.shape
    slots = cache_keys.shape[0]
    ctx_count = lax.axis_size("ctx")
    tp_count = lax.axis_size("tp")
    ctx_index = lax.axis_index("ctx")
    tp_index = lax.axis_index("tp")
    all_tokens = tokens * ctx_count

    def swap(block):
        return lax.ppermute(block, "ctx", [(i, i ^ 1) for i in range(ctx_count)])

    length = cache_lengths[0]
    digits = jnp.repeat(jnp.stack([length // 64, length % 64]), 8 * depth).reshape(16, depth)
    small = [
        jnp.concatenate(
            [
                new_keys.reshape(tokens, depth),
                new_values.reshape(tokens, depth),
                digits.astype(jnp.bfloat16),
            ],
            0,
        )
    ]
    keys = [cache_keys.reshape(slots, depth)]
    values = [cache_values.reshape(slots, depth)]
    for pair in (small, keys, values):
        pair.append(swap(pair[0]))
    other = small[1][2 * tokens, 0].astype(jnp.int32) * 64
    other = other + small[1][2 * tokens + 8, 0].astype(jnp.int32)
    facts = jnp.stack([causal_offset[0], length, other, ctx_index, ctx_index ^ 1])
    facts = facts.astype(jnp.int32)

    own = jnp.transpose(queries, (1, 0, 2))
    held = {(0, 0): (own, 0)}
    for rel in ((1, 0), (3, 0), (2, 0), (0, 1)):
        held[rel] = (fetch(own, rel, ctx_count), 0)
    far = jnp.concatenate([held[(i, 0)][0] for i in (1, 3, 2)], 0)
    far = fetch(far, (0, 1), ctx_count)
    for skip, i in enumerate((1, 3, 2)):
        held[(i, 1)] = (far, skip)

    packed = pack(facts, *keys, *values, *small, all_tokens)
    parts = []
    for call in CALLS:
        firsts = jnp.stack([chip_at(ctx_index, rel) * tokens for rel in call]).astype(jnp.int32)
        made = attend(
            facts, firsts, [held[rel][0] for rel in call], [held[rel][1] for rel in call], heads,
            *packed, slots, all_tokens,
        )
        for rel, part in zip(call, made):
            parts.append(part if rel == (0, 0) else deliver(part, rel, ctx_count))
    attended = merge(parts, tokens, heads * depth)

    blocks, spots = [], []
    for rel in ((0, 0),) + OTHERS:
        block = attended if rel == (0, 0) else fetch(attended, rel, ctx_count)
        blocks += [block, swap(block)]
        at = chip_at(ctx_index, rel)
        spots += [at, at ^ 1]
    spots += [tp_index ^ i for i in range(tp_count)]
    mixed = project(jnp.stack(spots).astype(jnp.int32), blocks, out_weight, tp_count)
    total = mixed[0].astype(jnp.float32)
    for i in range(1, tp_count):
        sent = lax.ppermute(mixed[i], "tp", [(j, j ^ i) for j in range(tp_count)])
        total = total + sent.astype(jnp.float32)
    return total


def solution(mesh):
    return jax.shard_map(
        local,
        mesh=mesh,
        in_specs=(
            P("ctx", "tp", None),
            P("ctx", "tp", None),
            P("ctx", "tp", None),
            P("ctx", "tp", None),
            P("ctx", "tp", None),
            P("ctx"),
            P(),
            P("tp", "ctx"),
        ),
        out_specs=P("tp", "ctx"),
        check_vma=False,
    )
```

```python
import functools
import math

import jax
import jax.numpy as jnp
from jax import lax
from jax.experimental import pallas as pl
from jax.experimental.pallas import tpu as pltpu
from jax.sharding import PartitionSpec as P

LOG2E = math.log2(math.e)
FAR = -1e30
NEVER = 1 << 30
CUT = 256
SMALL = 512
LARGE = 1024
VM = pl.BlockSpec(memory_space=pltpu.VMEM)
SM = pl.BlockSpec(memory_space=pltpu.SMEM)
EARLY = ((0,), (1, 3, 2))
LATE = ((2, 1), (3,), (0,))


def up16(n):
    return (n + 15) // 16 * 16


def spans(facts, slots, tokens):
    seen = [
        jnp.clip(jnp.minimum(facts[1 + s], facts[0] + tokens - facts[3 + s] * slots), 0, slots)
        for s in (0, 1)
    ]
    return seen, up16(seen[0]), up16(seen[1])


def collect_kernel(keys_ref, values_ref, new_keys_ref, new_values_ref, length, out_ref, sems):
    slots, depth = keys_ref.shape
    fresh = new_keys_ref.shape[0]
    copies = [
        pltpu.make_async_copy(src, out_ref.at[i * slots : (i + 1) * slots, :], sems.at[i])
        for i, src in enumerate((keys_ref, values_ref))
    ]
    for copy in copies:
        copy.start()
    at = 2 * slots
    out_ref[at : at + fresh, :] = new_keys_ref[...]
    out_ref[at + fresh : at + 2 * fresh, :] = new_values_ref[...]
    at += 2 * fresh
    for i, digit in enumerate((length[0] // 64, length[0] % 64)):
        line = jnp.full((8, depth), digit.astype(jnp.float32), jnp.float32)
        if i == 0:
            first = line
    out_ref[at : at + 16, :] = jnp.concatenate([first, line], 0).astype(out_ref.dtype)
    for copy in copies:
        copy.wait()


def collect(keys, values, new_keys, new_values, length):
    slots, depth = keys.shape
    far = pl.BlockSpec(memory_space=pltpu.HBM)
    return pl.pallas_call(
        collect_kernel,
        out_shape=jax.ShapeDtypeStruct(
            (2 * slots + 2 * new_keys.shape[0] + 16, depth), keys.dtype
        ),
        in_specs=[far, far, VM, VM, SM],
        out_specs=VM,
        scratch_shapes=[pltpu.SemaphoreType.DMA((2,))],
        compiler_params=pltpu.CompilerParams(vmem_limit_bytes=16 << 20),
        cost_estimate=pl.CostEstimate(
            flops=0, bytes_accessed=8 * slots * depth, transcendentals=0
        ),
    )(keys, values, new_keys, new_values, length)


def pack_kernel(tokens, slots, facts, all0, all1, keys_ref, values_ref, pos_ref, sems):
    fresh = (all0.shape[0] - 2 * slots - 16) // 2
    (n0, n1), c0, c1 = spans(facts, slots, tokens)
    outs = (keys_ref, values_ref)

    def move(pieces):
        copies = [
            pltpu.make_async_copy(
                src.at[start : start + size, :], out.at[pl.ds(at, size), :], sems.at[i]
            )
            for i, (src, start, size, out, at) in enumerate(pieces)
        ]
        for copy in copies:
            copy.start()
        for copy in copies:
            copy.wait()

    move([(all0, i * slots, slots, out, 0) for i, out in enumerate(outs)])
    at = pl.multiple_of(c0, 16)
    move([(all1, i * slots, slots, out, at) for i, out in enumerate(outs)])
    move(
        [
            (src, 2 * slots + i * fresh, fresh, out, pl.multiple_of(c0 + c1 + j * fresh, 16))
            for i, out in enumerate(outs)
            for j, src in enumerate((all0, all1))
        ]
    )
    for out in outs:
        at = pl.multiple_of(c0 + c1 + 2 * fresh, 16)
        out[pl.ds(at, SMALL), :] = jnp.zeros((SMALL, out.shape[1]), out.dtype)
    j = lax.broadcasted_iota(jnp.int32, pos_ref.shape, 1)
    one = j - c0
    two = one - c1
    three = two - fresh
    pos = jnp.where(j < n0, facts[3] * slots + j, NEVER)
    pos = jnp.where(j >= c0, jnp.where(one < n1, facts[4] * slots + one, NEVER), pos)
    pos = jnp.where(two >= 0, facts[0] + facts[3] * fresh + two, pos)
    pos = jnp.where(three >= 0, facts[0] + facts[4] * fresh + three, pos)
    pos = jnp.where(three >= fresh, NEVER, pos)
    pos_ref[...] = pos


def pack(facts, all0, all1, slots, tokens):
    depth = all0.shape[1]
    size = 2 * slots + (all0.shape[0] - 2 * slots - 16) + SMALL
    anywhere = pl.BlockSpec(memory_space=pl.ANY)
    return pl.pallas_call(
        functools.partial(pack_kernel, tokens, slots),
        out_shape=(
            jax.ShapeDtypeStruct((size, depth), all0.dtype),
            jax.ShapeDtypeStruct((size, depth), all0.dtype),
            jax.ShapeDtypeStruct((1, size), jnp.int32),
        ),
        in_specs=[SM, anywhere, anywhere],
        out_specs=(VM, VM, VM),
        scratch_shapes=[pltpu.SemaphoreType.DMA((4,))],
        compiler_params=pltpu.CompilerParams(vmem_limit_bytes=16 << 20),
        cost_estimate=pl.CostEstimate(
            flops=0, bytes_accessed=8 * slots * depth * 2, transcendentals=0
        ),
    )(facts, all0, all1)


def attend_kernel(all_tokens, slots, n_chunk, late, facts, firsts, *refs):
    def take(n):
        nonlocal refs
        got, refs = refs[:n], refs[n:]
        return got

    q_refs = take(n_chunk)
    keys_ref, values_ref, pos_ref = take(3)
    if late:
        had_flags, had_accs, had_tops = take(n_chunk), take(n_chunk), take(n_chunk)
        out_refs = take(n_chunk)
        q2, acc, top = take(3)
        accs, tops = [acc.at[c] for c in range(n_chunk)], [top.at[c] for c in range(n_chunk)]
    else:
        accs, tops = take(n_chunk), take(n_chunk)
        flag_ref, q2 = take(2)
    heads, tokens, depth = q_refs[0].shape
    rows = heads * tokens
    scale = LOG2E / math.sqrt(depth)
    (n0, n1), c0, c1 = spans(facts, slots, all_tokens)
    count = (c0 + c1 + 2 * tokens + SMALL - 1) // SMALL
    token = lax.broadcasted_iota(jnp.int32, (tokens, 128), 0)
    lasts = [
        jnp.concatenate([token + (facts[0] + firsts[c])] * (CUT // tokens), 0)
        for c in range(n_chunk)
    ]
    starts = [(c, r) for c in range(n_chunk) for r in range(0, rows, CUT)]

    def hide(scores, pos, last):
        return jnp.concatenate(
            [
                jnp.where(pos[:, at : at + 128] <= last, scores[:, at : at + 128], FAR)
                for at in range(0, scores.shape[1], 128)
            ],
            1,
        )

    def contract(left, right):
        return lax.dot_general(
            left, right, (((1,), (1,)), ((), ())), preferred_element_type=jnp.float32
        )

    def block_at(start, size):
        here = pl.ds(pl.multiple_of(start, SMALL), size)
        values = values_ref[here, :]
        return (
            keys_ref[here, :],
            jnp.concatenate([values, jnp.ones_like(values)], 1),
            pos_ref[:, here],
        )

    for c, r in starts:
        scaled = q_refs[c][r // tokens : (r + CUT) // tokens].reshape(CUT, depth)
        scaled = scaled.astype(jnp.float32) * scale
        high = scaled.astype(jnp.bfloat16)
        q2[c, r : r + CUT, :depth] = high
        q2[c, r : r + CUT, depth:] = (scaled - high.astype(jnp.float32)).astype(jnp.bfloat16)
    for c in range(n_chunk):
        accs[c][...] = had_accs[c][...] if late else jnp.zeros(accs[c].shape, jnp.float32)

    def step(start, size):
        keys, values, pos = block_at(start, size)
        keys = jnp.concatenate([keys, keys], 1)
        for c, r in starts:
            scores = hide(contract(q2[c, r : r + CUT, :], keys), pos, lasts[c])
            accs[c][r : r + CUT, :] += jnp.dot(
                jnp.exp2(scores).astype(jnp.bfloat16), values, preferred_element_type=jnp.float32
            )

    def large_step(at, _):
        step(at * LARGE, LARGE)
        return 0

    lax.fori_loop(0, count // 2, large_step, 0)

    @pl.when(count % 2 == 1)
    def _():
        step((count - 1) * SMALL, SMALL)

    groups = rows // 128
    eye = lax.broadcasted_iota(jnp.int32, (128, 128), 0) == lax.broadcasted_iota(
        jnp.int32, (128, 128), 1
    )

    def dense(ref, at):
        lines = []
        for g in range(groups):
            square = ref[g * 128 : (g + 1) * 128, at : at + 128]
            lines.append(jnp.sum(jnp.where(eye, square, 0.0), axis=0, keepdims=True))
        return jnp.concatenate(lines, 0)

    who = lax.broadcasted_iota(jnp.int32, (groups, 128), 1) % tokens
    wrong = jnp.zeros((groups, 128), jnp.float32)
    for c in range(n_chunk):
        total = dense(accs[c], depth)
        mine = who + firsts[c]
        seen = (mine >= facts[3] * tokens) | (mine >= facts[4] * tokens)
        for s, n in ((0, n0), (1, n1)):
            seen = seen | ((n > 0) & (mine + facts[0] >= facts[3 + s] * slots))
        sound = (total > 2.0**-100) & (total < 2.0**120)
        wrong = jnp.maximum(wrong, jnp.where(seen & ~sound, 1.0, 0.0))
        tops[c][...] = jnp.zeros(tops[c].shape, jnp.float32)
    general = jnp.max(wrong) > 0.0
    if late:
        for flag in had_flags:
            general = general | (flag[0] > 0)
    else:
        flag_ref[0] = general.astype(jnp.int32)

    @pl.when(general)
    def _():
        cuts = rows // CUT
        for c in range(n_chunk):
            if late:
                had = had_accs[c][:, depth:]
                accs[c][...] = had_accs[c][...]
                tops[c][...] = jnp.where(had > 0.0, had_tops[c][...], FAR)
            else:
                accs[c][...] = jnp.zeros(accs[c].shape, jnp.float32)
                tops[c][...] = jnp.full(tops[c].shape, FAR, jnp.float32)

            def slow_step(i, _):
                at, r = i // cuts, i % cuts
                keys, values, pos = block_at(at * SMALL, SMALL)
                per = CUT // tokens
                query = q_refs[c][pl.ds(r * per, per)].reshape(CUT, depth)
                scores = hide(contract(query, keys) * scale, pos, lasts[c])
                here = pl.ds(pl.multiple_of(r * CUT, CUT), CUT)
                old = tops[c][here, :]
                peak = jnp.maximum(old, jnp.max(scores, axis=1, keepdims=True))
                tops[c][here, :] = peak
                part = jnp.where(scores > FAR * 0.5, jnp.exp2(scores - peak[:, :1]), 0.0)
                fade = jnp.exp2(old - peak)
                accs[c][here, :] = accs[c][here, :] * jnp.concatenate([fade, fade], 1) + jnp.dot(
                    part.astype(jnp.bfloat16), values, preferred_element_type=jnp.float32
                )
                return 0

            lax.fori_loop(0, count * cuts, slow_step, 0)

    if not late:
        return
    for c, r in starts:
        some = accs[c][r : r + CUT, depth:]
        out_refs[c][r : r + CUT, :] = (
            accs[c][r : r + CUT, :depth] / jnp.where(some > 0.0, some, 1.0)
        ).astype(jnp.bfloat16)
    for c in range(n_chunk):
        total = dense(accs[c], depth)
        level = jnp.where(
            total > 0.0,
            dense(tops[c], 0) + jnp.log2(jnp.where(total > 0.0, total, 1.0)),
            FAR,
        )
        pieces = []
        for _ in range(3):
            pieces.append(level.astype(jnp.bfloat16).astype(jnp.float32))
            level = level - pieces[-1]
        pieces.append(jnp.zeros_like(level))
        tail = jnp.concatenate(pieces, 0)
        out_refs[c][rows : rows + 4 * groups, :] = tail.astype(jnp.bfloat16)


def attend(facts, firsts, queries, packed, slots, all_tokens, states=None):
    heads, tokens, depth = queries[0].shape
    rows = heads * tokens
    n = len(queries)
    late = states is not None
    scratch = [pltpu.VMEM((n, rows, 2 * depth), jnp.bfloat16)]
    if late:
        given = [state[i] for i in range(3) for state in states]
        given_specs = [SM] * n + [VM] * (2 * n)
        out_shape = [jax.ShapeDtypeStruct((rows + rows // 32, depth), jnp.bfloat16)] * n
        out_specs = [VM] * n
        scratch += [
            pltpu.VMEM((n, rows, 2 * depth), jnp.float32),
            pltpu.VMEM((n, rows, depth), jnp.float32),
        ]
    else:
        given, given_specs = [], []
        out_shape = [jax.ShapeDtypeStruct((rows, 2 * depth), jnp.float32)] * n
        out_shape += [jax.ShapeDtypeStruct((rows, depth), jnp.float32)] * n
        out_shape += [jax.ShapeDtypeStruct((1,), jnp.int32)]
        out_specs = [VM] * (2 * n) + [SM]
    made = pl.pallas_call(
        functools.partial(attend_kernel, all_tokens, slots, n, late),
        out_shape=out_shape,
        in_specs=[SM, SM] + [VM] * (n + 3) + given_specs,
        out_specs=out_specs,
        scratch_shapes=scratch,
        compiler_params=pltpu.CompilerParams(vmem_limit_bytes=28 << 20),
        cost_estimate=pl.CostEstimate(
            flops=2 * rows * n * packed[0].shape[0] * depth,
            bytes_accessed=4 * packed[0].shape[0] * depth,
            transcendentals=0,
        ),
    )(facts, firsts, *queries, *packed, *given)
    if late:
        return made
    return [(made[2 * n], made[c], made[n + c]) for c in range(n)]


def merge_kernel(*refs):
    parts, out_ref = refs[:-1], refs[-1]
    tokens = out_ref.shape[0]
    depth = parts[0].shape[1]
    rows = tokens * out_ref.shape[1] // depth
    groups = rows // 128
    levels = []
    for part in parts:
        tail = part[rows : rows + 4 * groups, :].astype(jnp.float32)
        levels.append(
            tail[:groups] + tail[groups : 2 * groups] + tail[2 * groups : 3 * groups]
        )
    peak = functools.reduce(jnp.maximum, levels)
    shares = [jnp.exp2(level - peak) for level in levels]
    total = functools.reduce(jnp.add, shares)
    shares = [share / total for share in shares]
    eye = lax.broadcasted_iota(jnp.int32, (128, 128), 0) == lax.broadcasted_iota(
        jnp.int32, (128, 128), 1
    )
    for g in range(groups):
        mix, blocks = [], []
        for share, part in zip(shares, parts):
            square = jnp.where(eye, share[g : g + 1, :], 0.0)
            high = square.astype(jnp.bfloat16)
            mix += [high, (square - high.astype(jnp.float32)).astype(jnp.bfloat16)]
            block = part[g * 128 : (g + 1) * 128, :]
            blocks += [block, block]
        merged = jnp.dot(
            jnp.concatenate(mix, 1), jnp.concatenate(blocks, 0), preferred_element_type=jnp.float32
        ).astype(out_ref.dtype)
        for i in range(128 // tokens):
            head = g * (128 // tokens) + i
            out_ref[:, head * depth : (head + 1) * depth] = merged[i * tokens : (i + 1) * tokens]


def merge(parts, tokens, width):
    return pl.pallas_call(
        merge_kernel,
        out_shape=jax.ShapeDtypeStruct((tokens, width), jnp.bfloat16),
        in_specs=[VM] * len(parts),
        out_specs=VM,
        compiler_params=pltpu.CompilerParams(vmem_limit_bytes=16 << 20),
        cost_estimate=pl.CostEstimate(
            flops=1 << 22, bytes_accessed=9 * tokens * width * 2, transcendentals=0
        ),
    )(*parts)


def project_kernel(n_block, spots, *refs):
    blocks, weight_ref = refs[:n_block], refs[n_block]
    out_refs = refs[n_block + 1 : -2]
    all_rows, mixed = refs[-2:]
    tokens = blocks[0].shape[0]
    for i, block in enumerate(blocks):
        all_rows[pl.ds(pl.multiple_of(spots[i] * tokens, tokens), tokens), :] = block[...]
    width = weight_ref.shape[1]
    for at in range(0, width, 256):
        mixed[:, at : at + 256] = jnp.dot(
            all_rows[...], weight_ref[:, at : at + 256], preferred_element_type=jnp.float32
        ).astype(mixed.dtype)
    tall = out_refs[0].shape[0]
    for i, out in enumerate(out_refs):
        out[...] = mixed[pl.ds(pl.multiple_of(spots[n_block + i] * tall, tall), tall), :]


def project(spots, blocks, weight, n_out):
    tokens, width = blocks[0].shape
    total = tokens * len(blocks)
    cols = weight.shape[1]
    return pl.pallas_call(
        functools.partial(project_kernel, len(blocks)),
        out_shape=[jax.ShapeDtypeStruct((total // n_out, cols), jnp.bfloat16)] * n_out,
        in_specs=[SM] + [VM] * (len(blocks) + 1),
        out_specs=[VM] * n_out,
        scratch_shapes=[
            pltpu.VMEM((total, width), jnp.bfloat16),
            pltpu.VMEM((total, cols), jnp.bfloat16),
        ],
        compiler_params=pltpu.CompilerParams(vmem_limit_bytes=28 << 20),
        cost_estimate=pl.CostEstimate(
            flops=2 * total * width * cols,
            bytes_accessed=2 * (total * width + width * cols + total * cols),
            transcendentals=0,
        ),
    )(spots, *blocks, weight)


def preload_kernel(weight_ref, after_ref, out_ref, sem):
    copy = pltpu.make_async_copy(weight_ref, out_ref, sem)
    copy.start()
    copy.wait()


def preload(weight, after):
    anywhere = pl.BlockSpec(memory_space=pl.ANY)
    far = pl.BlockSpec(memory_space=pltpu.HBM)
    return pl.pallas_call(
        preload_kernel,
        out_shape=jax.ShapeDtypeStruct(weight.shape, weight.dtype),
        in_specs=[far, anywhere],
        out_specs=VM,
        scratch_shapes=[pltpu.SemaphoreType.DMA],
        compiler_params=pltpu.CompilerParams(vmem_limit_bytes=16 << 20),
        cost_estimate=pl.CostEstimate(
            flops=0, bytes_accessed=4 * weight.size, transcendentals=0
        ),
    )(weight, after)


def chip_at(index, rel):
    z, y, core = index // 4, index // 2 % 2, index % 2
    return ((z + rel[0]) % 4 * 2 + (y + rel[1]) % 2) * 2 + core


def fetch(block, rel, count):
    return lax.ppermute(block, "ctx", [(chip_at(i, rel), i) for i in range(count)])


def deliver(block, rel, count):
    return lax.ppermute(block, "ctx", [(i, chip_at(i, rel)) for i in range(count)])


def local(
    queries, cache_keys, cache_values, new_keys, new_values, cache_lengths, causal_offset, out_weight
):
    tokens, heads, depth = queries.shape
    slots = cache_keys.shape[0]
    ctx_count = lax.axis_size("ctx")
    tp_count = lax.axis_size("tp")
    ctx_index = lax.axis_index("ctx")
    tp_index = lax.axis_index("tp")
    all_tokens = tokens * ctx_count

    def swap(block):
        return lax.ppermute(block, "ctx", [(i, i ^ 1) for i in range(ctx_count)])

    mine = collect(
        cache_keys.reshape(slots, depth),
        cache_values.reshape(slots, depth),
        new_keys.reshape(tokens, depth),
        new_values.reshape(tokens, depth),
        cache_lengths,
    )
    mate = swap(mine)
    far = fetch(mine, (0, 1), ctx_count)
    own = jnp.transpose(queries, (1, 0, 2))
    held = {0: own}
    for i in (1, 3, 2):
        held[i] = fetch(own, (i, 0), ctx_count)

    def after(blocks, state):
        return lax.optimization_barrier((tuple(blocks), state))[0]

    def prepare(one, two, place):
        at = 2 * slots + 2 * tokens
        lengths = [
            block[at, 0].astype(jnp.int32) * 64 + block[at + 8, 0].astype(jnp.int32)
            for block in (one, two)
        ]
        facts = jnp.stack([causal_offset[0], *lengths, place, place ^ 1]).astype(jnp.int32)
        return facts, pack(facts, one, two, slots, all_tokens)

    def work(call, prepared, states=None):
        firsts = jnp.stack([chip_at(ctx_index, (i, 0)) * tokens for i in call])
        facts, packed = prepared
        return attend(
            facts, firsts.astype(jnp.int32), [held[i] for i in call], packed, slots, all_tokens,
            states,
        )

    states = {}
    near = prepare(mine, mate, ctx_index)
    for call in EARLY:
        if 0 not in call:
            waited = after([held[i] for i in call], states[0][0])
            held.update(zip(call, waited))
        states.update(zip(call, work(call, near)))
    far = after([far], states[1][0])[0]
    away = prepare(far, swap(far), ctx_index ^ 2)
    parts = []
    for call in LATE:
        for i, part in zip(call, work(call, away, [states[i] for i in call])):
            parts.append(part if i == 0 else deliver(part, (i, 0), ctx_count))
    attended = merge(parts, tokens, heads * depth)
    weight = preload(out_weight, attended)

    blocks, spots = [], []
    for rel in [(i, j) for j in (0, 1) for i in (0, 2, 1, 3)]:
        block = attended if rel == (0, 0) else fetch(attended, rel, ctx_count)
        blocks += [block, swap(block)]
        at = chip_at(ctx_index, rel)
        spots += [at, at ^ 1]
    spots += [tp_index ^ i for i in range(tp_count)]
    mixed = project(jnp.stack(spots).astype(jnp.int32), blocks, weight, tp_count)
    total = mixed[0].astype(jnp.float32)
    for i in range(1, tp_count):
        sent = lax.ppermute(mixed[i], "tp", [(j, j ^ i) for j in range(tp_count)])
        total = total + sent.astype(jnp.float32)
    return total


def solution(mesh):
    return jax.shard_map(
        local,
        mesh=mesh,
        in_specs=(
            P("ctx", "tp", None),
            P("ctx", "tp", None),
            P("ctx", "tp", None),
            P("ctx", "tp", None),
            P("ctx", "tp", None),
            P("ctx"),
            P(),
            P("tp", "ctx"),
        ),
        out_specs=P("tp", "ctx"),
        check_vma=False,
    )
```

```python
import functools
import math

import jax
import jax.numpy as jnp
from jax import lax
from jax.experimental import pallas as pl
from jax.experimental.pallas import tpu as pltpu
from jax.sharding import PartitionSpec as P

LOG2E = math.log2(math.e)
FAR = -1e30
NEVER = 1 << 30
CUT = 256
SMALL = 512
LARGE = 1024
SCOPE = 24 << 20
VM = pl.BlockSpec(memory_space=pltpu.VMEM)
SM = pl.BlockSpec(memory_space=pltpu.SMEM)
EARLY = (0, 1, 3, 2)
LATE = ((2, 1), (3,), (0,))


def up16(n):
    return (n + 15) // 16 * 16


def spans(facts, slots, tokens):
    seen = [
        jnp.clip(jnp.minimum(facts[1 + s], facts[0] + tokens - facts[3 + s] * slots), 0, slots)
        for s in (0, 1)
    ]
    return seen, up16(seen[0]), up16(seen[1])


def collect_kernel(
    keys_ref, values_ref, new_keys_ref, new_values_ref, length, out_ref, small_ref, sems
):
    slots, depth = keys_ref.shape
    fresh = new_keys_ref.shape[0]
    copies = [
        pltpu.make_async_copy(src, out_ref.at[i * slots : (i + 1) * slots, :], sems.at[i])
        for i, src in enumerate((keys_ref, values_ref))
    ]
    for copy in copies:
        copy.start()
    lines = []
    for i, digit in enumerate((length[0] // 64, length[0] % 64)):
        lines.append(jnp.full((8, depth), digit.astype(jnp.float32), jnp.float32))
    for ref, at in ((out_ref, 2 * slots), (small_ref, 0)):
        ref[at : at + fresh, :] = new_keys_ref[...]
        ref[at + fresh : at + 2 * fresh, :] = new_values_ref[...]
        at += 2 * fresh
        ref[at : at + 16, :] = jnp.concatenate(lines, 0).astype(ref.dtype)
    for copy in copies:
        copy.wait()


def collect(keys, values, new_keys, new_values, length):
    slots, depth = keys.shape
    far = pl.BlockSpec(memory_space=pltpu.HBM)
    return pl.pallas_call(
        collect_kernel,
        out_shape=(
            jax.ShapeDtypeStruct((2 * slots + 2 * new_keys.shape[0] + 16, depth), keys.dtype),
            jax.ShapeDtypeStruct((2 * new_keys.shape[0] + 16, depth), keys.dtype),
        ),
        in_specs=[far, far, VM, VM, SM],
        out_specs=(VM, VM),
        scratch_shapes=[pltpu.SemaphoreType.DMA((2,))],
        compiler_params=pltpu.CompilerParams(vmem_limit_bytes=56 << 20),
        cost_estimate=pl.CostEstimate(
            flops=0, bytes_accessed=8 * slots * depth, transcendentals=0
        ),
    )(keys, values, new_keys, new_values, length)


def pack_kernel(tokens, slots, apart, offset, places, *refs):
    if apart:
        ones, refs = [(ref, 0) for ref in refs[:3]], refs[3:]
    else:
        ones, refs = [(refs[0], at) for at in (0, slots, 2 * slots)], refs[1:]
    twos = [(refs[0], at) for at in (0, slots, 2 * slots)]
    keys_ref, values_ref, pos_ref, facts_ref, digits, sems = refs[1:]
    fresh = (refs[0].shape[0] - 2 * slots - 16) // 2
    outs = (keys_ref, values_ref)

    def move(pieces):
        copies = [
            pltpu.make_async_copy(
                src.at[start : start + size, :], out.at[pl.ds(at, size), :], sems.at[i]
            )
            for i, (src, start, size, out, at) in enumerate(pieces)
        ]
        for copy in copies:
            copy.start()
        for copy in copies:
            copy.wait()

    move(
        [(src, at + 2 * fresh, 16, digits, 16 * i) for i, (src, at) in enumerate((ones[2], twos[2]))]
        + [(src, at, slots, out, 0) for (src, at), out in zip(ones, outs)]
    )
    told = digits[...].astype(jnp.float32)
    facts_ref[0] = offset[0]
    for i in (0, 1):
        high, low = jnp.max(told[16 * i : 16 * i + 8]), jnp.max(told[16 * i + 8 : 16 * i + 16])
        facts_ref[1 + i] = (high * 64.0 + low).astype(jnp.int32)
        facts_ref[3 + i] = places[i]
    facts = [facts_ref[i] for i in range(5)]
    (n0, n1), c0, c1 = spans(facts, slots, tokens)
    at = pl.multiple_of(c0, 16)
    move([(src, start, slots, out, at) for (src, start), out in zip(twos, outs)])
    move(
        [
            (src, start + i * fresh, fresh, out, pl.multiple_of(c0 + c1 + j * fresh, 16))
            for i, out in enumerate(outs)
            for j, (src, start) in enumerate((ones[2], twos[2]))
        ]
    )
    for out in outs:
        at = pl.multiple_of(c0 + c1 + 2 * fresh, 16)
        out[pl.ds(at, SMALL), :] = jnp.zeros((SMALL, out.shape[1]), out.dtype)
    j = lax.broadcasted_iota(jnp.int32, pos_ref.shape, 1)
    one = j - c0
    two = one - c1
    three = two - fresh
    pos = jnp.where(j < n0, facts[3] * slots + j, NEVER)
    pos = jnp.where(j >= c0, jnp.where(one < n1, facts[4] * slots + one, NEVER), pos)
    pos = jnp.where(two >= 0, facts[0] + facts[3] * fresh + two, pos)
    pos = jnp.where(three >= 0, facts[0] + facts[4] * fresh + three, pos)
    pos = jnp.where(three >= fresh, NEVER, pos)
    pos_ref[...] = pos


def pack(offset, places, ones, all1, slots, tokens):
    depth = all1.shape[1]
    size = 2 * slots + (all1.shape[0] - 2 * slots - 16) + SMALL
    anywhere = pl.BlockSpec(memory_space=pl.ANY)
    return pl.pallas_call(
        functools.partial(pack_kernel, tokens, slots, len(ones) > 1),
        out_shape=(
            jax.ShapeDtypeStruct((size, depth), all1.dtype),
            jax.ShapeDtypeStruct((size, depth), all1.dtype),
            jax.ShapeDtypeStruct((1, size), jnp.int32),
            jax.ShapeDtypeStruct((8,), jnp.int32),
        ),
        in_specs=[SM, SM] + [anywhere] * (len(ones) + 1),
        out_specs=(VM, VM, VM, SM),
        scratch_shapes=[pltpu.VMEM((32, depth), all1.dtype), pltpu.SemaphoreType.DMA((4,))],
        compiler_params=pltpu.CompilerParams(vmem_limit_bytes=12 << 20),
        cost_estimate=pl.CostEstimate(
            flops=0, bytes_accessed=8 * slots * depth * 2, transcendentals=0
        ),
    )(offset, places, *ones, all1)


def attend_kernel(all_tokens, slots, n_chunk, late, firsts, *refs):
    def take(n):
        nonlocal refs
        got, refs = refs[:n], refs[n:]
        return got

    q_refs = take(n_chunk)
    passes = [take(4)]
    if late:
        had_accs = take(n_chunk)
        passes.append(take(4))
        out_refs = take(n_chunk)
        q2, acc, top = refs
        accs, tops = [acc.at[c] for c in range(n_chunk)], [top.at[c] for c in range(n_chunk)]
    else:
        accs = take(n_chunk)
        (q2,) = refs
    heads, tokens, depth = q_refs[0].shape
    rows = heads * tokens
    scale = LOG2E / math.sqrt(depth)
    offset = passes[0][3][0]

    def count_of(facts):
        _, c0, c1 = spans(facts, slots, all_tokens)
        return (c0 + c1 + 2 * tokens + SMALL - 1) // SMALL

    token = lax.broadcasted_iota(jnp.int32, (tokens, 128), 0)
    lasts = [
        jnp.concatenate([token + (offset + firsts[c])] * (CUT // tokens), 0)
        for c in range(n_chunk)
    ]
    starts = [(c, r) for c in range(n_chunk) for r in range(0, rows, CUT)]

    def hide(scores, pos, last):
        return jnp.concatenate(
            [
                jnp.where(pos[:, at : at + 128] <= last, scores[:, at : at + 128], FAR)
                for at in range(0, scores.shape[1], 128)
            ],
            1,
        )

    def contract(left, right):
        return lax.dot_general(
            left, right, (((1,), (1,)), ((), ())), preferred_element_type=jnp.float32
        )

    def block_at(refs, start, size):
        keys_ref, values_ref, pos_ref, _ = refs
        here = pl.ds(pl.multiple_of(start, SMALL), size)
        values = values_ref[here, :]
        return (
            keys_ref[here, :],
            jnp.concatenate([values, jnp.ones_like(values)], 1),
            pos_ref[:, here],
        )

    for c, r in starts:
        scaled = q_refs[c][r // tokens : (r + CUT) // tokens].reshape(CUT, depth)
        scaled = scaled.astype(jnp.float32) * scale
        high = scaled.astype(jnp.bfloat16)
        q2[c, r : r + CUT, :depth] = high
        q2[c, r : r + CUT, depth:] = (scaled - high.astype(jnp.float32)).astype(jnp.bfloat16)
    for c in range(n_chunk):
        accs[c][...] = had_accs[c][...] if late else jnp.zeros(accs[c].shape, jnp.float32)
    count = count_of(passes[0][3])

    def step(start, size):
        keys, values, pos = block_at(passes[0], start, size)
        keys = jnp.concatenate([keys, keys], 1)
        for c, r in starts:
            scores = hide(contract(q2[c, r : r + CUT, :], keys), pos, lasts[c])
            accs[c][r : r + CUT, :] += jnp.dot(
                jnp.exp2(scores).astype(jnp.bfloat16), values, preferred_element_type=jnp.float32
            )

    def large_step(at, _):
        step(at * LARGE, LARGE)
        return 0

    lax.fori_loop(0, count // 2, large_step, 0)

    @pl.when(count % 2 == 1)
    def _():
        step((count - 1) * SMALL, SMALL)

    if not late:
        return
    groups = rows // 128
    eye = lax.broadcasted_iota(jnp.int32, (128, 128), 0) == lax.broadcasted_iota(
        jnp.int32, (128, 128), 1
    )

    def dense(ref, at):
        lines = []
        for g in range(groups):
            square = ref[g * 128 : (g + 1) * 128, at : at + 128]
            lines.append(jnp.sum(jnp.where(eye, square, 0.0), axis=0, keepdims=True))
        return jnp.concatenate(lines, 0)

    who = lax.broadcasted_iota(jnp.int32, (groups, 128), 1) % tokens
    wrong = jnp.zeros((groups, 128), jnp.float32)
    for c in range(n_chunk):
        total = dense(accs[c], depth)
        mine = who + firsts[c]
        seen = jnp.zeros((groups, 128), jnp.bool_)
        for _, _, _, facts in passes:
            counts, _, _ = spans(facts, slots, all_tokens)
            for s in (0, 1):
                seen = seen | (mine >= facts[3 + s] * tokens)
                seen = seen | ((counts[s] > 0) & (mine + offset >= facts[3 + s] * slots))
        sound = (total > 2.0**-100) & (total < 2.0**120)
        wrong = jnp.maximum(wrong, jnp.where(seen & ~sound, 1.0, 0.0))
        tops[c][...] = jnp.zeros(tops[c].shape, jnp.float32)

    @pl.when(jnp.max(wrong) > 0.0)
    def _():
        cuts = rows // CUT
        for c in range(n_chunk):
            accs[c][...] = jnp.zeros(accs[c].shape, jnp.float32)
            tops[c][...] = jnp.full(tops[c].shape, FAR, jnp.float32)
            for refs in passes:

                def slow_step(i, _):
                    at, r = i // cuts, i % cuts
                    keys, values, pos = block_at(refs, at * SMALL, SMALL)
                    per = CUT // tokens
                    query = q_refs[c][pl.ds(r * per, per)].reshape(CUT, depth)
                    scores = hide(contract(query, keys) * scale, pos, lasts[c])
                    here = pl.ds(pl.multiple_of(r * CUT, CUT), CUT)
                    old = tops[c][here, :]
                    peak = jnp.maximum(old, jnp.max(scores, axis=1, keepdims=True))
                    tops[c][here, :] = peak
                    part = jnp.where(scores > FAR * 0.5, jnp.exp2(scores - peak[:, :1]), 0.0)
                    fade = jnp.exp2(old - peak)
                    accs[c][here, :] = accs[c][here, :] * jnp.concatenate(
                        [fade, fade], 1
                    ) + jnp.dot(
                        part.astype(jnp.bfloat16), values, preferred_element_type=jnp.float32
                    )
                    return 0

                lax.fori_loop(0, count_of(refs[3]) * cuts, slow_step, 0)

    for c, r in starts:
        some = accs[c][r : r + CUT, depth:]
        out_refs[c][r : r + CUT, :] = (
            accs[c][r : r + CUT, :depth] / jnp.where(some > 0.0, some, 1.0)
        ).astype(jnp.bfloat16)
    for c in range(n_chunk):
        total = dense(accs[c], depth)
        level = jnp.where(
            total > 0.0,
            dense(tops[c], 0) + jnp.log2(jnp.where(total > 0.0, total, 1.0)),
            FAR,
        )
        pieces = []
        for _ in range(3):
            pieces.append(level.astype(jnp.bfloat16).astype(jnp.float32))
            level = level - pieces[-1]
        pieces.append(jnp.zeros_like(level))
        tail = jnp.concatenate(pieces, 0)
        out_refs[c][rows : rows + 4 * groups, :] = tail.astype(jnp.bfloat16)


def attend(firsts, queries, packed, slots, all_tokens, states=None, before=None):
    heads, tokens, depth = queries[0].shape
    rows = heads * tokens
    n = len(queries)
    late = states is not None
    scratch = [pltpu.VMEM((n, rows, 2 * depth), jnp.bfloat16)]
    packed_specs = [VM, VM, VM, SM]
    given, given_specs = [], []
    if late:
        given, given_specs = [*states, *before], [VM] * n + packed_specs
        out_shape = [jax.ShapeDtypeStruct((rows + rows // 32, depth), jnp.bfloat16)] * n
        scratch += [
            pltpu.VMEM((n, rows, 2 * depth), jnp.float32),
            pltpu.VMEM((n, rows, depth), jnp.float32),
        ]
    else:
        out_shape = [jax.ShapeDtypeStruct((rows, 2 * depth), jnp.float32)] * n
    return pl.pallas_call(
        functools.partial(attend_kernel, all_tokens, slots, n, late),
        out_shape=out_shape,
        in_specs=[SM] + [VM] * n + packed_specs + given_specs,
        out_specs=[VM] * n,
        scratch_shapes=scratch,
        compiler_params=pltpu.CompilerParams(vmem_limit_bytes=SCOPE),
        cost_estimate=pl.CostEstimate(
            flops=2 * rows * n * packed[0].shape[0] * depth,
            bytes_accessed=4 * packed[0].shape[0] * depth,
            transcendentals=0,
        ),
    )(firsts, *queries, *packed, *given)


def merge_kernel(*refs):
    parts, out_ref = refs[:-1], refs[-1]
    tokens = out_ref.shape[0]
    depth = parts[0].shape[1]
    rows = tokens * out_ref.shape[1] // depth
    groups = rows // 128
    levels = []
    for part in parts:
        tail = part[rows : rows + 4 * groups, :].astype(jnp.float32)
        levels.append(
            tail[:groups] + tail[groups : 2 * groups] + tail[2 * groups : 3 * groups]
        )
    peak = functools.reduce(jnp.maximum, levels)
    shares = [jnp.exp2(level - peak) for level in levels]
    total = functools.reduce(jnp.add, shares)
    shares = [share / total for share in shares]
    eye = lax.broadcasted_iota(jnp.int32, (128, 128), 0) == lax.broadcasted_iota(
        jnp.int32, (128, 128), 1
    )
    for g in range(groups):
        mix, blocks = [], []
        for share, part in zip(shares, parts):
            square = jnp.where(eye, share[g : g + 1, :], 0.0)
            high = square.astype(jnp.bfloat16)
            mix += [high, (square - high.astype(jnp.float32)).astype(jnp.bfloat16)]
            block = part[g * 128 : (g + 1) * 128, :]
            blocks += [block, block]
        merged = jnp.dot(
            jnp.concatenate(mix, 1), jnp.concatenate(blocks, 0), preferred_element_type=jnp.float32
        ).astype(out_ref.dtype)
        for i in range(128 // tokens):
            head = g * (128 // tokens) + i
            out_ref[:, head * depth : (head + 1) * depth] = merged[i * tokens : (i + 1) * tokens]


def merge(parts, tokens, width):
    return pl.pallas_call(
        merge_kernel,
        out_shape=jax.ShapeDtypeStruct((tokens, width), jnp.bfloat16),
        in_specs=[VM] * len(parts),
        out_specs=VM,
        compiler_params=pltpu.CompilerParams(vmem_limit_bytes=16 << 20),
        cost_estimate=pl.CostEstimate(
            flops=1 << 22, bytes_accessed=9 * tokens * width * 2, transcendentals=0
        ),
    )(*parts)


def project_kernel(n_block, spots, *refs):
    blocks, weight_ref = refs[:n_block], refs[n_block]
    out_refs = refs[n_block + 1 : -2]
    all_rows, mixed = refs[-2:]
    tokens = blocks[0].shape[0]
    for i, block in enumerate(blocks):
        all_rows[pl.ds(pl.multiple_of(spots[i] * tokens, tokens), tokens), :] = block[...]
    width = weight_ref.shape[1]
    for at in range(0, width, 256):
        mixed[:, at : at + 256] = jnp.dot(
            all_rows[...], weight_ref[:, at : at + 256], preferred_element_type=jnp.float32
        ).astype(mixed.dtype)
    tall = out_refs[0].shape[0]
    for i, out in enumerate(out_refs):
        out[...] = mixed[pl.ds(pl.multiple_of(spots[n_block + i] * tall, tall), tall), :]


def project(spots, blocks, weight, n_out):
    tokens, width = blocks[0].shape
    total = tokens * len(blocks)
    cols = weight.shape[1]
    return pl.pallas_call(
        functools.partial(project_kernel, len(blocks)),
        out_shape=[jax.ShapeDtypeStruct((total // n_out, cols), jnp.bfloat16)] * n_out,
        in_specs=[SM] + [VM] * (len(blocks) + 1),
        out_specs=[VM] * n_out,
        scratch_shapes=[
            pltpu.VMEM((total, width), jnp.bfloat16),
            pltpu.VMEM((total, cols), jnp.bfloat16),
        ],
        compiler_params=pltpu.CompilerParams(vmem_limit_bytes=28 << 20),
        cost_estimate=pl.CostEstimate(
            flops=2 * total * width * cols,
            bytes_accessed=2 * (total * width + width * cols + total * cols),
            transcendentals=0,
        ),
    )(spots, *blocks, weight)


def chip_at(index, rel):
    z, y, core = index // 4, index // 2 % 2, index % 2
    return ((z + rel[0]) % 4 * 2 + (y + rel[1]) % 2) * 2 + core


def fetch(block, rel, count):
    return lax.ppermute(block, "ctx", [(chip_at(i, rel), i) for i in range(count)])


def deliver(block, rel, count):
    return lax.ppermute(block, "ctx", [(i, chip_at(i, rel)) for i in range(count)])


def local(
    queries, cache_keys, cache_values, new_keys, new_values, cache_lengths, causal_offset, out_weight
):
    tokens, heads, depth = queries.shape
    slots = cache_keys.shape[0]
    ctx_count = lax.axis_size("ctx")
    tp_count = lax.axis_size("tp")
    ctx_index = lax.axis_index("ctx")
    tp_index = lax.axis_index("tp")
    all_tokens = tokens * ctx_count

    def swap(block):
        return lax.ppermute(block, "ctx", [(i, i ^ 1) for i in range(ctx_count)])

    keys, values = cache_keys.reshape(slots, depth), cache_values.reshape(slots, depth)
    mine, small = collect(
        keys,
        values,
        new_keys.reshape(tokens, depth),
        new_values.reshape(tokens, depth),
        cache_lengths,
    )
    mate = swap(mine)
    far = fetch(mine, (0, 1), ctx_count)
    own = jnp.transpose(queries, (1, 0, 2))
    held = {0: own}
    for i in (1, 3, 2):
        held[i] = fetch(own, (i, 0), ctx_count)

    def after(blocks, state):
        return lax.optimization_barrier((tuple(blocks), state))[0]

    def prepare(ones, two, place):
        places = jnp.stack([place, place ^ 1]).astype(jnp.int32)
        return pack(causal_offset, places, ones, two, slots, all_tokens)

    def work(call, packed, states=None, before=None):
        firsts = jnp.stack([chip_at(ctx_index, (i, 0)) * tokens for i in call])
        return attend(
            firsts.astype(jnp.int32), [held[i] for i in call], packed, slots, all_tokens, states,
            before,
        )

    near = prepare((keys, values, small), mate, ctx_index)
    states = dict(zip(EARLY, work(EARLY, near)))
    far = after([far], states[0])[0]
    away = prepare((far,), swap(far), ctx_index ^ 2)
    parts = []
    for call in LATE:
        for i, part in zip(call, work(call, away, [states[i] for i in call], near)):
            parts.append(part if i == 0 else deliver(part, (i, 0), ctx_count))
    attended = merge(parts, tokens, heads * depth)

    blocks, spots = [], []
    for rel in [(i, j) for j in (0, 1) for i in (0, 2, 1, 3)]:
        block = attended if rel == (0, 0) else fetch(attended, rel, ctx_count)
        blocks += [block, swap(block)]
        at = chip_at(ctx_index, rel)
        spots += [at, at ^ 1]
    spots += [tp_index ^ i for i in range(tp_count)]
    mixed = project(jnp.stack(spots).astype(jnp.int32), blocks, out_weight, tp_count)
    total = mixed[0].astype(jnp.float32)
    for i in (6, 4, 5, 7, 2, 1, 3):
        sent = lax.ppermute(mixed[i], "tp", [(j, j ^ i) for j in range(tp_count)])
        total = total + sent.astype(jnp.float32)
    return total


def solution(mesh):
    return jax.shard_map(
        local,
        mesh=mesh,
        in_specs=(
            P("ctx", "tp", None),
            P("ctx", "tp", None),
            P("ctx", "tp", None),
            P("ctx", "tp", None),
            P("ctx", "tp", None),
            P("ctx"),
            P(),
            P("tp", "ctx"),
        ),
        out_specs=P("tp", "ctx"),
        check_vma=False,
    )
```

```python
import functools
import math

import jax
import jax.numpy as jnp
from jax import lax
from jax.experimental import pallas as pl
from jax.experimental.pallas import tpu as pltpu
from jax.sharding import PartitionSpec as P

LOG2E = math.log2(math.e)
FAR = -1e30
NEVER = 1 << 30
CUT = 256
SMALL = 512
LARGE = 1024
SCOPE = 14 << 20
VM = pl.BlockSpec(memory_space=pltpu.VMEM)
SM = pl.BlockSpec(memory_space=pltpu.SMEM)
EARLY = ((0,), (2, 1, 3))
LATE = ((2, 1, 3), (0,))


def up16(n):
    return (n + 15) // 16 * 16


def spans(facts, slots, tokens):
    seen = [
        jnp.clip(jnp.minimum(facts[1 + s], facts[0] + tokens - facts[3 + s] * slots), 0, slots)
        for s in (0, 1)
    ]
    return seen, up16(seen[0]), up16(seen[1])


def collect_kernel(keys_ref, values_ref, new_keys_ref, new_values_ref, length, out_ref, sems):
    slots, depth = keys_ref.shape
    fresh = new_keys_ref.shape[0]
    copies = [
        pltpu.make_async_copy(src, out_ref.at[i * slots : (i + 1) * slots, :], sems.at[i])
        for i, src in enumerate((keys_ref, values_ref))
    ]
    for copy in copies:
        copy.start()
    at = 2 * slots
    out_ref[at : at + fresh, :] = new_keys_ref[...]
    out_ref[at + fresh : at + 2 * fresh, :] = new_values_ref[...]
    at += 2 * fresh
    for i, digit in enumerate((length[0] // 64, length[0] % 64)):
        line = jnp.full((8, depth), digit.astype(jnp.float32), jnp.float32)
        if i == 0:
            first = line
    out_ref[at : at + 16, :] = jnp.concatenate([first, line], 0).astype(out_ref.dtype)
    for copy in copies:
        copy.wait()


def collect(keys, values, new_keys, new_values, length):
    slots, depth = keys.shape
    far = pl.BlockSpec(memory_space=pltpu.HBM)
    return pl.pallas_call(
        collect_kernel,
        out_shape=jax.ShapeDtypeStruct(
            (2 * slots + 2 * new_keys.shape[0] + 16, depth), keys.dtype
        ),
        in_specs=[far, far, VM, VM, SM],
        out_specs=VM,
        scratch_shapes=[pltpu.SemaphoreType.DMA((2,))],
        compiler_params=pltpu.CompilerParams(vmem_limit_bytes=4 << 20),
        cost_estimate=pl.CostEstimate(
            flops=0, bytes_accessed=8 * slots * depth, transcendentals=0
        ),
    )(keys, values, new_keys, new_values, length)


def pack_kernel(
    tokens, slots, offset, places, all0, all1, keys_ref, values_ref, pos_ref, facts_ref, digits, sems
):
    fresh = (all0.shape[0] - 2 * slots - 16) // 2
    outs = (keys_ref, values_ref)

    def move(pieces):
        copies = [
            pltpu.make_async_copy(
                src.at[start : start + size, :], out.at[pl.ds(at, size), :], sems.at[i]
            )
            for i, (src, start, size, out, at) in enumerate(pieces)
        ]
        for copy in copies:
            copy.start()
        for copy in copies:
            copy.wait()

    at = 2 * slots + 2 * fresh
    move([(src, at, 16, digits, 16 * i) for i, src in enumerate((all0, all1))])
    move([(all0, i * slots, slots, out, 0) for i, out in enumerate(outs)])
    told = digits[...].astype(jnp.float32)
    facts_ref[0] = offset[0]
    for i in (0, 1):
        high, low = jnp.max(told[16 * i : 16 * i + 8]), jnp.max(told[16 * i + 8 : 16 * i + 16])
        facts_ref[1 + i] = (high * 64.0 + low).astype(jnp.int32)
        facts_ref[3 + i] = places[i]
    facts = [facts_ref[i] for i in range(5)]
    (n0, n1), c0, c1 = spans(facts, slots, tokens)
    at = pl.multiple_of(c0, 16)
    move([(all1, i * slots, slots, out, at) for i, out in enumerate(outs)])
    move(
        [
            (src, 2 * slots + i * fresh, fresh, out, pl.multiple_of(c0 + c1 + j * fresh, 16))
            for i, out in enumerate(outs)
            for j, src in enumerate((all0, all1))
        ]
    )
    for out in outs:
        at = pl.multiple_of(c0 + c1 + 2 * fresh, 16)
        out[pl.ds(at, SMALL), :] = jnp.zeros((SMALL, out.shape[1]), out.dtype)
    j = lax.broadcasted_iota(jnp.int32, pos_ref.shape, 1)
    one = j - c0
    two = one - c1
    three = two - fresh
    pos = jnp.where(j < n0, facts[3] * slots + j, NEVER)
    pos = jnp.where(j >= c0, jnp.where(one < n1, facts[4] * slots + one, NEVER), pos)
    pos = jnp.where(two >= 0, facts[0] + facts[3] * fresh + two, pos)
    pos = jnp.where(three >= 0, facts[0] + facts[4] * fresh + three, pos)
    pos = jnp.where(three >= fresh, NEVER, pos)
    pos_ref[...] = pos


def pack(offset, places, all0, all1, slots, tokens):
    depth = all0.shape[1]
    size = 2 * slots + (all0.shape[0] - 2 * slots - 16) + SMALL
    anywhere = pl.BlockSpec(memory_space=pl.ANY)
    return pl.pallas_call(
        functools.partial(pack_kernel, tokens, slots),
        out_shape=(
            jax.ShapeDtypeStruct((size, depth), all0.dtype),
            jax.ShapeDtypeStruct((size, depth), all0.dtype),
            jax.ShapeDtypeStruct((1, size), jnp.int32),
            jax.ShapeDtypeStruct((8,), jnp.int32),
        ),
        in_specs=[SM, SM, anywhere, anywhere],
        out_specs=(VM, VM, VM, SM),
        scratch_shapes=[pltpu.VMEM((32, depth), all0.dtype), pltpu.SemaphoreType.DMA((4,))],
        compiler_params=pltpu.CompilerParams(vmem_limit_bytes=4 << 20),
        cost_estimate=pl.CostEstimate(
            flops=0, bytes_accessed=8 * slots * depth * 2, transcendentals=0
        ),
    )(offset, places, all0, all1)


def attend_kernel(all_tokens, slots, n_chunk, late, firsts, *refs):
    q_refs, refs = refs[:n_chunk], refs[n_chunk:]
    keys_ref, values_ref, pos_ref, facts = refs[:4]
    refs = refs[4:]
    if late:
        had_refs, refs = refs[:n_chunk], refs[n_chunk:]
    out_refs, (q2, acc, top, tops) = refs[:n_chunk], refs[n_chunk:]
    heads, tokens, depth = q_refs[0].shape
    rows = heads * tokens
    scale = LOG2E / math.sqrt(depth)
    (n0, n1), c0, c1 = spans(facts, slots, all_tokens)
    count = (c0 + c1 + 2 * tokens + SMALL - 1) // SMALL
    token = lax.broadcasted_iota(jnp.int32, (tokens, 128), 0)
    lasts = [
        jnp.concatenate([token + (facts[0] + firsts[c])] * (CUT // tokens), 0)
        for c in range(n_chunk)
    ]
    starts = [(c, r) for c in range(n_chunk) for r in range(0, rows, CUT)]

    def hide(scores, pos, last):
        return jnp.concatenate(
            [
                jnp.where(pos[:, at : at + 128] <= last, scores[:, at : at + 128], FAR)
                for at in range(0, scores.shape[1], 128)
            ],
            1,
        )

    def contract(left, right):
        return lax.dot_general(
            left, right, (((1,), (1,)), ((), ())), preferred_element_type=jnp.float32
        )

    def block_at(start, size):
        here = pl.ds(pl.multiple_of(start, SMALL), size)
        values = values_ref[here, :]
        return (
            keys_ref[here, :],
            jnp.concatenate([values, jnp.ones_like(values)], 1),
            pos_ref[:, here],
        )

    for c, r in starts:
        scaled = q_refs[c][r // tokens : (r + CUT) // tokens].reshape(CUT, depth)
        scaled = scaled.astype(jnp.float32) * scale
        high = scaled.astype(jnp.bfloat16)
        q2[c, r : r + CUT, :depth] = high
        q2[c, r : r + CUT, depth:] = (scaled - high.astype(jnp.float32)).astype(jnp.bfloat16)
    acc[...] = jnp.zeros_like(acc)

    def step(start, size):
        keys, values, pos = block_at(start, size)
        keys = jnp.concatenate([keys, keys], 1)
        for c, r in starts:
            scores = hide(contract(q2[c, r : r + CUT, :], keys), pos, lasts[c])
            acc[c, r : r + CUT, :] += jnp.dot(
                jnp.exp2(scores).astype(jnp.bfloat16), values, preferred_element_type=jnp.float32
            )

    def large_step(at, _):
        step(at * LARGE, LARGE)
        return 0

    lax.fori_loop(0, count // 2, large_step, 0)

    @pl.when(count % 2 == 1)
    def _():
        step((count - 1) * SMALL, SMALL)

    groups = rows // 128
    eye = lax.broadcasted_iota(jnp.int32, (128, 128), 0) == lax.broadcasted_iota(
        jnp.int32, (128, 128), 1
    )

    def dense(ref, at):
        lines = []
        for g in range(groups):
            square = ref[g * 128 : (g + 1) * 128, at : at + 128]
            lines.append(jnp.sum(jnp.where(eye, square, 0.0), axis=0, keepdims=True))
        return jnp.concatenate(lines, 0)

    who = lax.broadcasted_iota(jnp.int32, (groups, 128), 1) % tokens
    wrong = jnp.zeros((groups, 128), jnp.float32)
    for c in range(n_chunk):
        total = dense(acc.at[c], depth)
        mine = who + firsts[c]
        seen = (mine >= facts[3] * tokens) | (mine >= facts[4] * tokens)
        for s, n in ((0, n0), (1, n1)):
            seen = seen | ((n > 0) & (mine + facts[0] >= facts[3 + s] * slots))
        sound = (total > 2.0**-100) & (total < 2.0**120)
        wrong = jnp.maximum(wrong, jnp.where(seen & ~sound, 1.0, 0.0))
    tops[...] = jnp.zeros_like(tops)

    @pl.when(jnp.max(wrong) > 0.0)
    def _():
        acc[...] = jnp.zeros_like(acc)
        cuts = rows // CUT
        for c in range(n_chunk):
            top[...] = jnp.full_like(top, FAR)

            def slow_step(i, _):
                at, r = i // cuts, i % cuts
                keys, values, pos = block_at(at * SMALL, SMALL)
                per = CUT // tokens
                query = q_refs[c][pl.ds(r * per, per)].reshape(CUT, depth)
                scores = hide(contract(query, keys) * scale, pos, lasts[c])
                here = pl.ds(pl.multiple_of(r * CUT, CUT), CUT)
                old = top[here, :]
                peak = jnp.maximum(old, jnp.max(scores, axis=1, keepdims=True))
                top[here, :] = peak
                part = jnp.where(scores > FAR * 0.5, jnp.exp2(scores - peak[:, :1]), 0.0)
                fade = jnp.exp2(old - peak)
                acc[c, here, :] = acc[c, here, :] * jnp.concatenate([fade, fade], 1) + jnp.dot(
                    part.astype(jnp.bfloat16), values, preferred_element_type=jnp.float32
                )
                return 0

            lax.fori_loop(0, count * cuts, slow_step, 0)
            tops[c] = dense(top, 0)

    def split(line):
        square = jnp.where(eye, line, 0.0)
        high = square.astype(jnp.bfloat16)
        return jnp.concatenate([high, (square - high.astype(jnp.float32)).astype(jnp.bfloat16)], 1)

    for c in range(n_chunk):
        total = dense(acc.at[c], depth)
        level = jnp.where(
            total > 0.0,
            tops[c] + jnp.log2(jnp.where(total > 0.0, total, 1.0)),
            FAR,
        )
        if late:
            tail = had_refs[c][rows : rows + 4 * groups, :].astype(jnp.float32)
            other = tail[:groups] + tail[groups : 2 * groups] + tail[2 * groups : 3 * groups]
            peak = jnp.maximum(level, other)
            shares = [jnp.exp2(level - peak), jnp.exp2(other - peak)]
            whole = shares[0] + shares[1]
            level = peak + jnp.log2(whole)
            shares = [share / whole for share in shares]
        for g in range(groups):
            here = slice(g * 128, (g + 1) * 128)
            some = acc[c, here, depth:]
            fresh = acc[c, here, :depth] / jnp.where(some > 0.0, some, 1.0)
            if late:
                block = had_refs[c][here, :]
                fresh = fresh * jnp.dot(
                    split(shares[0][g : g + 1, :]),
                    jnp.ones((256, 128), jnp.bfloat16),
                    preferred_element_type=jnp.float32,
                ) + jnp.dot(
                    split(shares[1][g : g + 1, :]),
                    jnp.concatenate([block, block], 0),
                    preferred_element_type=jnp.float32,
                )
            out_refs[c][here, :] = fresh.astype(jnp.bfloat16)
        pieces = []
        for _ in range(3):
            pieces.append(level.astype(jnp.bfloat16).astype(jnp.float32))
            level = level - pieces[-1]
        pieces.append(jnp.zeros_like(level))
        tail = jnp.concatenate(pieces, 0)
        out_refs[c][rows : rows + 4 * groups, :] = tail.astype(jnp.bfloat16)


def attend(firsts, queries, packed, slots, all_tokens, had=()):
    heads, tokens, depth = queries[0].shape
    rows = heads * tokens
    n = len(queries)
    return pl.pallas_call(
        functools.partial(attend_kernel, all_tokens, slots, n, bool(had)),
        out_shape=[jax.ShapeDtypeStruct((rows + rows // 32, depth), jnp.bfloat16)] * n,
        in_specs=[SM] + [VM] * (n + 3) + [SM] + [VM] * len(had),
        out_specs=[VM] * n,
        scratch_shapes=[
            pltpu.VMEM((n, rows, 2 * depth), jnp.bfloat16),
            pltpu.VMEM((n, rows, 2 * depth), jnp.float32),
            pltpu.VMEM((rows, depth), jnp.float32),
            pltpu.VMEM((n, rows // 128, 128), jnp.float32),
        ],
        compiler_params=pltpu.CompilerParams(vmem_limit_bytes=SCOPE),
        cost_estimate=pl.CostEstimate(
            flops=2 * rows * n * packed[0].shape[0] * depth,
            bytes_accessed=4 * packed[0].shape[0] * depth,
            transcendentals=0,
        ),
    )(firsts, *queries, *packed, *had)


def merge_kernel(*refs):
    parts, out_ref = refs[:-1], refs[-1]
    tokens = out_ref.shape[0]
    depth = parts[0].shape[1]
    rows = tokens * out_ref.shape[1] // depth
    groups = rows // 128
    levels = []
    for part in parts:
        tail = part[rows : rows + 4 * groups, :].astype(jnp.float32)
        levels.append(
            tail[:groups] + tail[groups : 2 * groups] + tail[2 * groups : 3 * groups]
        )
    peak = functools.reduce(jnp.maximum, levels)
    shares = [jnp.exp2(level - peak) for level in levels]
    total = functools.reduce(jnp.add, shares)
    shares = [share / total for share in shares]
    eye = lax.broadcasted_iota(jnp.int32, (128, 128), 0) == lax.broadcasted_iota(
        jnp.int32, (128, 128), 1
    )
    for g in range(groups):
        mix, blocks = [], []
        for share, part in zip(shares, parts):
            square = jnp.where(eye, share[g : g + 1, :], 0.0)
            high = square.astype(jnp.bfloat16)
            mix += [high, (square - high.astype(jnp.float32)).astype(jnp.bfloat16)]
            block = part[g * 128 : (g + 1) * 128, :]
            blocks += [block, block]
        merged = jnp.dot(
            jnp.concatenate(mix, 1), jnp.concatenate(blocks, 0), preferred_element_type=jnp.float32
        ).astype(out_ref.dtype)
        for i in range(128 // tokens):
            head = g * (128 // tokens) + i
            out_ref[:, head * depth : (head + 1) * depth] = merged[i * tokens : (i + 1) * tokens]


def merge(parts, tokens, width):
    return pl.pallas_call(
        merge_kernel,
        out_shape=jax.ShapeDtypeStruct((tokens, width), jnp.bfloat16),
        in_specs=[VM] * len(parts),
        out_specs=VM,
        compiler_params=pltpu.CompilerParams(vmem_limit_bytes=4 << 20),
        cost_estimate=pl.CostEstimate(
            flops=1 << 22, bytes_accessed=9 * tokens * width * 2, transcendentals=0
        ),
    )(*parts)


def project_kernel(n_block, early, spots, *refs):
    blocks, weight_ref = refs[:n_block], refs[n_block]
    refs = refs[n_block + 1 :]
    out_ref, rows = refs[-2:]
    tokens = blocks[0].shape[0]
    for i, block in enumerate(blocks):
        rows[i * tokens : (i + 1) * tokens, :] = block[...]

    def place(i, at, part):
        here = pl.ds(pl.multiple_of(spots[i] * tokens, tokens), tokens)
        out_ref[here, at : at + part.shape[1]] = part

    if early:
        for i in range(refs[0].shape[0] // tokens):
            place(n_block + i, 0, refs[0][i * tokens : (i + 1) * tokens, :])
    for at in range(0, weight_ref.shape[1], 256):
        part = jnp.dot(
            rows[...], weight_ref[:, at : at + 256], preferred_element_type=jnp.float32
        ).astype(out_ref.dtype)
        if early:
            for i in range(n_block):
                place(i, at, part[i * tokens : (i + 1) * tokens, :])
        else:
            out_ref[:, at : at + 256] = part


def project(spots, blocks, weight, early=None):
    tokens = blocks[0].shape[0]
    total = tokens * len(blocks)
    width, cols = weight.shape
    given = [] if early is None else [early]
    out_rows = total + (0 if early is None else early.shape[0])
    return pl.pallas_call(
        functools.partial(project_kernel, len(blocks), early is not None),
        out_shape=jax.ShapeDtypeStruct((out_rows, cols), jnp.bfloat16),
        in_specs=[SM] + [VM] * (len(blocks) + 1 + len(given)),
        out_specs=VM,
        scratch_shapes=[pltpu.VMEM((total, width), jnp.bfloat16)],
        compiler_params=pltpu.CompilerParams(vmem_limit_bytes=20 << 20),
        cost_estimate=pl.CostEstimate(
            flops=2 * total * width * cols,
            bytes_accessed=2 * (total * width + width * cols + out_rows * cols),
            transcendentals=0,
        ),
    )(spots, *blocks, weight, *given)


def chip_at(index, rel):
    z, y, core = index // 4, index // 2 % 2, index % 2
    return ((z + rel[0]) % 4 * 2 + (y + rel[1]) % 2) * 2 + core


def fetch(block, rel, count):
    return lax.ppermute(block, "ctx", [(chip_at(i, rel), i) for i in range(count)])


def deliver(block, rel, count):
    return lax.ppermute(block, "ctx", [(i, chip_at(i, rel)) for i in range(count)])


def local(
    queries, cache_keys, cache_values, new_keys, new_values, cache_lengths, causal_offset, out_weight
):
    tokens, heads, depth = queries.shape
    slots = cache_keys.shape[0]
    ctx_count = lax.axis_size("ctx")
    tp_count = lax.axis_size("tp")
    ctx_index = lax.axis_index("ctx")
    all_tokens = tokens * ctx_count

    def swap(block):
        return lax.ppermute(block, "ctx", [(i, i ^ 1) for i in range(ctx_count)])

    mine = collect(
        cache_keys.reshape(slots, depth),
        cache_values.reshape(slots, depth),
        new_keys.reshape(tokens, depth),
        new_values.reshape(tokens, depth),
        cache_lengths,
    )
    mate = swap(mine)
    far = fetch(mine, (0, 1), ctx_count)
    own = jnp.transpose(queries, (1, 0, 2))
    held = {0: own}
    for i in (1, 3, 2):
        held[i] = fetch(own, (i, 0), ctx_count)

    def after(blocks, state):
        return lax.optimization_barrier((tuple(blocks), state))[0]

    def prepare(one, two, place):
        places = jnp.stack([place, place ^ 1]).astype(jnp.int32)
        return pack(causal_offset, places, one, two, slots, all_tokens)

    parts = {}

    def work(calls, packed):
        for call in calls:
            firsts = jnp.stack([chip_at(ctx_index, (i, 0)) * tokens for i in call])
            had = [parts[i] for i in call if i in parts]
            made = attend(
                firsts.astype(jnp.int32), [held[i] for i in call], packed, slots, all_tokens, had
            )
            parts.update(zip(call, made))
        return made[0]

    near = prepare(mine, mate, ctx_index)
    last = work(EARLY[:1], near)
    held.update(zip((1, 2, 3), after([held[i] for i in (1, 2, 3)], last)))
    last = work(EARLY[1:], near)
    far = after([far], last)[0]
    work(LATE, prepare(far, swap(far), ctx_index ^ 2))
    parts = [part if i == 0 else deliver(part, (i, 0), ctx_count) for i, part in parts.items()]
    attended = merge(parts, tokens, heads * depth)

    halves = []
    for rels in (((0, 0), (0, 1), (1, 0), (3, 0)), ((2, 1), (1, 1), (3, 1), (2, 0))):
        blocks, spots = [], []
        for rel in rels:
            block = attended if rel == (0, 0) else fetch(attended, rel, ctx_count)
            blocks += [block, swap(block)]
            at = chip_at(ctx_index, rel)
            spots += [at, at ^ 1]
        halves.append((blocks, spots))
    spots = jnp.stack(halves[1][1] + halves[0][1]).astype(jnp.int32)
    early = project(spots, halves[0][0], out_weight)
    mixed = project(spots, halves[1][0], out_weight, early)
    shares = lax.all_to_all(mixed, "tp", 0, 0, tiled=True)
    return jnp.sum(shares.reshape(tp_count, -1, mixed.shape[1]).astype(jnp.float32), axis=0)


def solution(mesh):
    return jax.shard_map(
        local,
        mesh=mesh,
        in_specs=(
            P("ctx", "tp", None),
            P("ctx", "tp", None),
            P("ctx", "tp", None),
            P("ctx", "tp", None),
            P("ctx", "tp", None),
            P("ctx"),
            P(),
            P("tp", "ctx"),
        ),
        out_specs=P("tp", "ctx"),
        check_vma=False,
    )
```

```python
import functools
import math

import jax
import jax.numpy as jnp
from jax import lax
from jax.experimental import pallas as pl
from jax.experimental.pallas import tpu as pltpu
from jax.sharding import PartitionSpec as P

LOG2E = math.log2(math.e)
FAR = -1e30
NEVER = 1 << 30
CUT = 256
SMALL = 512
LARGE = 1024
SCOPE = 14 << 20
VM = pl.BlockSpec(memory_space=pltpu.VMEM)
SM = pl.BlockSpec(memory_space=pltpu.SMEM)
EARLY = ((0,), (2, 1, 3))
LATE = ((2, 1, 3), (0,))


def up16(n):
    return (n + 15) // 16 * 16


def spans(facts, slots, tokens):
    seen = [
        jnp.clip(jnp.minimum(facts[1 + s], facts[0] + tokens - facts[3 + s] * slots), 0, slots)
        for s in (0, 1)
    ]
    return seen, up16(seen[0]), up16(seen[1])


def collect_kernel(keys_ref, values_ref, new_keys_ref, new_values_ref, length, out_ref, sems):
    slots, depth = keys_ref.shape
    fresh = new_keys_ref.shape[0]
    copies = [
        pltpu.make_async_copy(src, out_ref.at[i * slots : (i + 1) * slots, :], sems.at[i])
        for i, src in enumerate((keys_ref, values_ref))
    ]
    for copy in copies:
        copy.start()
    at = 2 * slots
    out_ref[at : at + fresh, :] = new_keys_ref[...]
    out_ref[at + fresh : at + 2 * fresh, :] = new_values_ref[...]
    at += 2 * fresh
    for i, digit in enumerate((length[0] // 64, length[0] % 64)):
        line = jnp.full((8, depth), digit.astype(jnp.float32), jnp.float32)
        if i == 0:
            first = line
    out_ref[at : at + 16, :] = jnp.concatenate([first, line], 0).astype(out_ref.dtype)
    for copy in copies:
        copy.wait()


def collect(keys, values, new_keys, new_values, length):
    slots, depth = keys.shape
    far = pl.BlockSpec(memory_space=pltpu.HBM)
    return pl.pallas_call(
        collect_kernel,
        out_shape=jax.ShapeDtypeStruct(
            (2 * slots + 2 * new_keys.shape[0] + 16, depth), keys.dtype
        ),
        in_specs=[far, far, VM, VM, SM],
        out_specs=VM,
        scratch_shapes=[pltpu.SemaphoreType.DMA((2,))],
        compiler_params=pltpu.CompilerParams(vmem_limit_bytes=4 << 20),
        cost_estimate=pl.CostEstimate(
            flops=0, bytes_accessed=8 * slots * depth, transcendentals=0
        ),
    )(keys, values, new_keys, new_values, length)


def pack_kernel(
    tokens, slots, offset, places, all0, all1, keys_ref, values_ref, pos_ref, facts_ref, digits, sems
):
    fresh = (all0.shape[0] - 2 * slots - 16) // 2
    outs = (keys_ref, values_ref)

    def move(pieces):
        copies = [
            pltpu.make_async_copy(
                src.at[start : start + size, :], out.at[pl.ds(at, size), :], sems.at[i]
            )
            for i, (src, start, size, out, at) in enumerate(pieces)
        ]
        for copy in copies:
            copy.start()
        for copy in copies:
            copy.wait()

    at = 2 * slots + 2 * fresh
    move([(src, at, 16, digits, 16 * i) for i, src in enumerate((all0, all1))])
    move([(all0, i * slots, slots, out, 0) for i, out in enumerate(outs)])
    told = digits[...].astype(jnp.float32)
    facts_ref[0] = offset[0]
    for i in (0, 1):
        high, low = jnp.max(told[16 * i : 16 * i + 8]), jnp.max(told[16 * i + 8 : 16 * i + 16])
        facts_ref[1 + i] = (high * 64.0 + low).astype(jnp.int32)
        facts_ref[3 + i] = places[i]
    facts = [facts_ref[i] for i in range(5)]
    (n0, n1), c0, c1 = spans(facts, slots, tokens)
    at = pl.multiple_of(c0, 16)
    move([(all1, i * slots, slots, out, at) for i, out in enumerate(outs)])
    move(
        [
            (src, 2 * slots + i * fresh, fresh, out, pl.multiple_of(c0 + c1 + j * fresh, 16))
            for i, out in enumerate(outs)
            for j, src in enumerate((all0, all1))
        ]
    )
    for out in outs:
        at = pl.multiple_of(c0 + c1 + 2 * fresh, 16)
        out[pl.ds(at, SMALL), :] = jnp.zeros((SMALL, out.shape[1]), out.dtype)
    j = lax.broadcasted_iota(jnp.int32, pos_ref.shape, 1)
    one = j - c0
    two = one - c1
    three = two - fresh
    pos = jnp.where(j < n0, facts[3] * slots + j, NEVER)
    pos = jnp.where(j >= c0, jnp.where(one < n1, facts[4] * slots + one, NEVER), pos)
    pos = jnp.where(two >= 0, facts[0] + facts[3] * fresh + two, pos)
    pos = jnp.where(three >= 0, facts[0] + facts[4] * fresh + three, pos)
    pos = jnp.where(three >= fresh, NEVER, pos)
    pos_ref[...] = pos


def pack(offset, places, all0, all1, slots, tokens):
    depth = all0.shape[1]
    size = 2 * slots + (all0.shape[0] - 2 * slots - 16) + SMALL
    anywhere = pl.BlockSpec(memory_space=pl.ANY)
    return pl.pallas_call(
        functools.partial(pack_kernel, tokens, slots),
        out_shape=(
            jax.ShapeDtypeStruct((size, depth), all0.dtype),
            jax.ShapeDtypeStruct((size, depth), all0.dtype),
            jax.ShapeDtypeStruct((1, size), jnp.int32),
            jax.ShapeDtypeStruct((8,), jnp.int32),
        ),
        in_specs=[SM, SM, anywhere, anywhere],
        out_specs=(VM, VM, VM, SM),
        scratch_shapes=[pltpu.VMEM((32, depth), all0.dtype), pltpu.SemaphoreType.DMA((4,))],
        compiler_params=pltpu.CompilerParams(vmem_limit_bytes=4 << 20),
        cost_estimate=pl.CostEstimate(
            flops=0, bytes_accessed=8 * slots * depth * 2, transcendentals=0
        ),
    )(offset, places, all0, all1)


def attend_kernel(all_tokens, slots, n_chunk, late, held_at, firsts, *refs):
    q_refs, refs = refs[:n_chunk], refs[n_chunk:]
    keys_ref, values_ref, pos_ref, facts = refs[:4]
    refs = refs[4:]
    tall = refs[-1].shape[1] * 128 + refs[-1].shape[1] * 4
    if late:
        had_refs = [ref.at[at * tall : (at + 1) * tall] for ref, at in zip(refs, held_at)]
        out_refs, (q2, acc, top, tops) = refs[n_chunk:-4], refs[-4:]
    else:
        out_ref, q2, acc, top, tops = refs
        out_refs = [out_ref.at[c * tall : (c + 1) * tall] for c in range(n_chunk)]
    heads, tokens, depth = q_refs[0].shape
    rows = heads * tokens
    scale = LOG2E / math.sqrt(depth)
    (n0, n1), c0, c1 = spans(facts, slots, all_tokens)
    count = (c0 + c1 + 2 * tokens + SMALL - 1) // SMALL
    token = lax.broadcasted_iota(jnp.int32, (tokens, 128), 0)
    lasts = [
        jnp.concatenate([token + (facts[0] + firsts[c])] * (CUT // tokens), 0)
        for c in range(n_chunk)
    ]
    starts = [(c, r) for c in range(n_chunk) for r in range(0, rows, CUT)]

    def hide(scores, pos, last):
        return jnp.concatenate(
            [
                jnp.where(pos[:, at : at + 128] <= last, scores[:, at : at + 128], FAR)
                for at in range(0, scores.shape[1], 128)
            ],
            1,
        )

    def contract(left, right):
        return lax.dot_general(
            left, right, (((1,), (1,)), ((), ())), preferred_element_type=jnp.float32
        )

    def block_at(start, size):
        here = pl.ds(pl.multiple_of(start, SMALL), size)
        values = values_ref[here, :]
        return (
            keys_ref[here, :],
            jnp.concatenate([values, jnp.ones_like(values)], 1),
            pos_ref[:, here],
        )

    for c, r in starts:
        scaled = q_refs[c][r // tokens : (r + CUT) // tokens].reshape(CUT, depth)
        scaled = scaled.astype(jnp.float32) * scale
        high = scaled.astype(jnp.bfloat16)
        q2[c, r : r + CUT, :depth] = high
        q2[c, r : r + CUT, depth:] = (scaled - high.astype(jnp.float32)).astype(jnp.bfloat16)
    acc[...] = jnp.zeros_like(acc)

    def step(start, size):
        keys, values, pos = block_at(start, size)
        keys = jnp.concatenate([keys, keys], 1)
        for c, r in starts:
            scores = hide(contract(q2[c, r : r + CUT, :], keys), pos, lasts[c])
            acc[c, r : r + CUT, :] += jnp.dot(
                jnp.exp2(scores).astype(jnp.bfloat16), values, preferred_element_type=jnp.float32
            )

    size = LARGE * 2 if n_chunk == 1 else LARGE

    def large_step(at, _):
        step(at * size, size)
        return 0

    lax.fori_loop(0, count // (size // SMALL), large_step, 0)
    rest = size // 2
    while rest >= SMALL:

        @pl.when(count // (rest // SMALL) % 2 == 1)
        def _(rest=rest):
            step(count // (2 * rest // SMALL) * (2 * rest), rest)

        rest //= 2

    groups = rows // 128
    eye = lax.broadcasted_iota(jnp.int32, (128, 128), 0) == lax.broadcasted_iota(
        jnp.int32, (128, 128), 1
    )

    def dense(ref, at):
        lines = []
        for g in range(groups):
            square = ref[g * 128 : (g + 1) * 128, at : at + 128]
            lines.append(jnp.sum(jnp.where(eye, square, 0.0), axis=0, keepdims=True))
        return jnp.concatenate(lines, 0)

    who = lax.broadcasted_iota(jnp.int32, (groups, 128), 1) % tokens
    wrong = jnp.zeros((groups, 128), jnp.float32)
    for c in range(n_chunk):
        total = dense(acc.at[c], depth)
        mine = who + firsts[c]
        seen = (mine >= facts[3] * tokens) | (mine >= facts[4] * tokens)
        for s, n in ((0, n0), (1, n1)):
            seen = seen | ((n > 0) & (mine + facts[0] >= facts[3 + s] * slots))
        sound = (total > 2.0**-100) & (total < 2.0**120)
        wrong = jnp.maximum(wrong, jnp.where(seen & ~sound, 1.0, 0.0))
    tops[...] = jnp.zeros_like(tops)

    @pl.when(jnp.max(wrong) > 0.0)
    def _():
        acc[...] = jnp.zeros_like(acc)
        cuts = rows // CUT
        for c in range(n_chunk):
            top[...] = jnp.full_like(top, FAR)

            def slow_step(i, _):
                at, r = i // cuts, i % cuts
                keys, values, pos = block_at(at * SMALL, SMALL)
                per = CUT // tokens
                query = q_refs[c][pl.ds(r * per, per)].reshape(CUT, depth)
                scores = hide(contract(query, keys) * scale, pos, lasts[c])
                here = pl.ds(pl.multiple_of(r * CUT, CUT), CUT)
                old = top[here, :]
                peak = jnp.maximum(old, jnp.max(scores, axis=1, keepdims=True))
                top[here, :] = peak
                part = jnp.where(scores > FAR * 0.5, jnp.exp2(scores - peak[:, :1]), 0.0)
                fade = jnp.exp2(old - peak)
                acc[c, here, :] = acc[c, here, :] * jnp.concatenate([fade, fade], 1) + jnp.dot(
                    part.astype(jnp.bfloat16), values, preferred_element_type=jnp.float32
                )
                return 0

            lax.fori_loop(0, count * cuts, slow_step, 0)
            tops[c] = dense(top, 0)

    def split(line):
        square = jnp.where(eye, line, 0.0)
        high = square.astype(jnp.bfloat16)
        return jnp.concatenate([high, (square - high.astype(jnp.float32)).astype(jnp.bfloat16)], 1)

    for c in range(n_chunk):
        total = dense(acc.at[c], depth)
        level = jnp.where(
            total > 0.0,
            tops[c] + jnp.log2(jnp.where(total > 0.0, total, 1.0)),
            FAR,
        )
        if late:
            tail = had_refs[c][rows : rows + 4 * groups, :].astype(jnp.float32)
            other = tail[:groups] + tail[groups : 2 * groups] + tail[2 * groups : 3 * groups]
            peak = jnp.maximum(level, other)
            shares = [jnp.exp2(level - peak), jnp.exp2(other - peak)]
            whole = shares[0] + shares[1]
            level = peak + jnp.log2(whole)
            shares = [share / whole for share in shares]
        for g in range(groups):
            here = slice(g * 128, (g + 1) * 128)
            some = acc[c, here, depth:]
            fresh = acc[c, here, :depth] / jnp.where(some > 0.0, some, 1.0)
            if late:
                block = had_refs[c][here, :]
                fresh = fresh * jnp.dot(
                    split(shares[0][g : g + 1, :]),
                    jnp.ones((256, 128), jnp.bfloat16),
                    preferred_element_type=jnp.float32,
                ) + jnp.dot(
                    split(shares[1][g : g + 1, :]),
                    jnp.concatenate([block, block], 0),
                    preferred_element_type=jnp.float32,
                )
            out_refs[c][here, :] = fresh.astype(jnp.bfloat16)
        pieces = []
        for _ in range(3):
            pieces.append(level.astype(jnp.bfloat16).astype(jnp.float32))
            level = level - pieces[-1]
        pieces.append(jnp.zeros_like(level))
        tail = jnp.concatenate(pieces, 0)
        out_refs[c][rows : rows + 4 * groups, :] = tail.astype(jnp.bfloat16)


def attend(firsts, queries, packed, slots, all_tokens, had=()):
    heads, tokens, depth = queries[0].shape
    rows = heads * tokens
    n = len(queries)
    tall = rows + rows // 32
    held_at = tuple(at for _, at in had)
    if had:
        shapes, specs = [jax.ShapeDtypeStruct((tall, depth), jnp.bfloat16)] * n, [VM] * n
    else:
        shapes, specs = jax.ShapeDtypeStruct((n * tall, depth), jnp.bfloat16), VM
    return pl.pallas_call(
        functools.partial(attend_kernel, all_tokens, slots, n, bool(had), held_at),
        out_shape=shapes,
        in_specs=[SM] + [VM] * (n + 3) + [SM] + [VM] * len(had),
        out_specs=specs,
        scratch_shapes=[
            pltpu.VMEM((n, rows, 2 * depth), jnp.bfloat16),
            pltpu.VMEM((n, rows, 2 * depth), jnp.float32),
            pltpu.VMEM((rows, depth), jnp.float32),
            pltpu.VMEM((n, rows // 128, 128), jnp.float32),
        ],
        compiler_params=pltpu.CompilerParams(vmem_limit_bytes=SCOPE),
        cost_estimate=pl.CostEstimate(
            flops=2 * rows * n * packed[0].shape[0] * depth,
            bytes_accessed=4 * packed[0].shape[0] * depth,
            transcendentals=0,
        ),
    )(firsts, *queries, *packed, *(block for block, _ in had))


def merge_kernel(*refs):
    parts, out_ref = refs[:-1], refs[-1]
    tokens = out_ref.shape[0]
    depth = parts[0].shape[1]
    rows = tokens * out_ref.shape[1] // depth
    groups = rows // 128
    levels = []
    for part in parts:
        tail = part[rows : rows + 4 * groups, :].astype(jnp.float32)
        levels.append(
            tail[:groups] + tail[groups : 2 * groups] + tail[2 * groups : 3 * groups]
        )
    peak = functools.reduce(jnp.maximum, levels)
    shares = [jnp.exp2(level - peak) for level in levels]
    total = functools.reduce(jnp.add, shares)
    shares = [share / total for share in shares]
    eye = lax.broadcasted_iota(jnp.int32, (128, 128), 0) == lax.broadcasted_iota(
        jnp.int32, (128, 128), 1
    )
    for g in range(groups):
        mix, blocks = [], []
        for share, part in zip(shares, parts):
            square = jnp.where(eye, share[g : g + 1, :], 0.0)
            high = square.astype(jnp.bfloat16)
            mix += [high, (square - high.astype(jnp.float32)).astype(jnp.bfloat16)]
            block = part[g * 128 : (g + 1) * 128, :]
            blocks += [block, block]
        merged = jnp.dot(
            jnp.concatenate(mix, 1), jnp.concatenate(blocks, 0), preferred_element_type=jnp.float32
        ).astype(out_ref.dtype)
        for i in range(128 // tokens):
            head = g * (128 // tokens) + i
            out_ref[:, head * depth : (head + 1) * depth] = merged[i * tokens : (i + 1) * tokens]


def merge(parts, tokens, width):
    return pl.pallas_call(
        merge_kernel,
        out_shape=jax.ShapeDtypeStruct((tokens, width), jnp.bfloat16),
        in_specs=[VM] * len(parts),
        out_specs=VM,
        compiler_params=pltpu.CompilerParams(vmem_limit_bytes=4 << 20),
        cost_estimate=pl.CostEstimate(
            flops=1 << 22, bytes_accessed=9 * tokens * width * 2, transcendentals=0
        ),
    )(*parts)


def project_kernel(n_block, tokens, spots, *refs):
    blocks, weight_ref = refs[:n_block], refs[n_block]
    out_ref, all_rows = refs[n_block + 1 :]
    i = 0
    for block in blocks:
        for at in range(0, block.shape[0], tokens):
            here = pl.ds(pl.multiple_of(spots[i] * tokens, tokens), tokens)
            all_rows[here, :] = block[at : at + tokens, :]
            i += 1
    for at in range(0, weight_ref.shape[1], 256):
        out_ref[:, at : at + 256] = jnp.dot(
            all_rows[...], weight_ref[:, at : at + 256], preferred_element_type=jnp.float32
        ).astype(out_ref.dtype)


def project(spots, blocks, weight, tokens):
    total = sum(block.shape[0] for block in blocks)
    width, cols = weight.shape
    return pl.pallas_call(
        functools.partial(project_kernel, len(blocks), tokens),
        out_shape=jax.ShapeDtypeStruct((total, cols), jnp.bfloat16),
        in_specs=[SM] + [VM] * (len(blocks) + 1),
        out_specs=VM,
        scratch_shapes=[pltpu.VMEM((total, width), jnp.bfloat16)],
        compiler_params=pltpu.CompilerParams(vmem_limit_bytes=12 << 20),
        cost_estimate=pl.CostEstimate(
            flops=2 * total * width * cols,
            bytes_accessed=2 * (total * width + width * cols + total * cols),
            transcendentals=0,
        ),
    )(spots, *blocks, weight)


def chip_at(index, rel):
    z, y, core = index // 4, index // 2 % 2, index % 2
    return ((z + rel[0]) % 4 * 2 + (y + rel[1]) % 2) * 2 + core


def fetch(block, rel, count):
    return lax.ppermute(block, "ctx", [(chip_at(i, rel), i) for i in range(count)])


def deliver(block, rel, count):
    return lax.ppermute(block, "ctx", [(i, chip_at(i, rel)) for i in range(count)])


def local(
    queries, cache_keys, cache_values, new_keys, new_values, cache_lengths, causal_offset, out_weight
):
    tokens, heads, depth = queries.shape
    slots = cache_keys.shape[0]
    ctx_count = lax.axis_size("ctx")
    tp_count = lax.axis_size("tp")
    ctx_index = lax.axis_index("ctx")
    all_tokens = tokens * ctx_count

    def swap(block):
        return lax.ppermute(block, "ctx", [(i, i ^ 1) for i in range(ctx_count)])

    mine = collect(
        cache_keys.reshape(slots, depth),
        cache_values.reshape(slots, depth),
        new_keys.reshape(tokens, depth),
        new_values.reshape(tokens, depth),
        cache_lengths,
    )
    mate = swap(mine)
    far = fetch(mine, (0, 1), ctx_count)
    own = jnp.transpose(queries, (1, 0, 2))
    held = {0: own}
    for i in (1, 3, 2):
        held[i] = fetch(own, (i, 0), ctx_count)

    def after(blocks, state):
        return lax.optimization_barrier((tuple(blocks), state))[0]

    def prepare(one, two, place):
        places = jnp.stack([place, place ^ 1]).astype(jnp.int32)
        return pack(causal_offset, places, one, two, slots, all_tokens)

    parts = {}

    def work(calls, packed):
        for call in calls:
            firsts = jnp.stack([chip_at(ctx_index, (i, 0)) * tokens for i in call])
            had = [parts[i] for i in call if i in parts]
            made = attend(
                firsts.astype(jnp.int32), [held[i] for i in call], packed, slots, all_tokens, had
            )
            if had:
                parts.update(zip(call, made))
            else:
                parts.update((i, (made, at)) for at, i in enumerate(call))
        return made

    near = prepare(mine, mate, ctx_index)
    last = work(EARLY[:1], near)
    held.update(zip((1, 2, 3), after([held[i] for i in (1, 2, 3)], last)))
    last = work(EARLY[1:], near)
    far = after([far], last)[0]
    work(LATE, prepare(far, swap(far), ctx_index ^ 2))
    parts = [part if i == 0 else deliver(part, (i, 0), ctx_count) for i, part in parts.items()]
    attended = merge(parts, tokens, heads * depth)

    blocks, spots = [], []
    for rel in ((0, 0), (0, 1), (1, 0), (3, 0), (2, 1), (1, 1), (3, 1), (2, 0)):
        block = attended if rel == (0, 0) else fetch(attended, rel, ctx_count)
        blocks += [block, swap(block)]
        at = chip_at(ctx_index, rel)
        spots += [at, at ^ 1]
    mixed = project(jnp.stack(spots).astype(jnp.int32), blocks, out_weight, tokens)
    shares = lax.all_to_all(mixed, "tp", 0, 0, tiled=True)
    return jnp.sum(shares.reshape(tp_count, -1, mixed.shape[1]).astype(jnp.float32), axis=0)


def solution(mesh):
    return jax.shard_map(
        local,
        mesh=mesh,
        in_specs=(
            P("ctx", "tp", None),
            P("ctx", "tp", None),
            P("ctx", "tp", None),
            P("ctx", "tp", None),
            P("ctx", "tp", None),
            P("ctx"),
            P(),
            P("tp", "ctx"),
        ),
        out_specs=P("tp", "ctx"),
        check_vma=False,
    )
```
